32 devices in a mesh: band: 16 (over z, y, core), pair: 2 (over x).
Axes of the slice: x: 2, y: 2, z: 4, core: 2. Of those that a mesh axis runs over, the one named last changes fastest.
Arguments:
- frame1: bfloat16 [16, 768, 256], P('band', 'pair'), parts along dimension 1, may hold values from -6 to 6, as said below
- frame2: bfloat16 [16, 768, 256], P('band', 'pair'), parts along dimension 1, may hold values from -6 to 6, as said below
- context: bfloat16 [16, 768, 128], P('band', 'pair'), parts along dimension 1, may hold values from -6 to 6
- hidden_init: bfloat16 [16, 768, 128], P('band', 'pair'), parts along dimension 1, may hold values from -1 to 1
- offsets: int32 [2, 16, 768], P(None, 'band', 'pair'), parts along dimension 2, may hold values from -4 to 4
- w_motion: float32 [3, 128], replicated, may hold values from -3.5 to 3.5
- w_row: bfloat16 [5, 384, 384], replicated, may hold values from -0.125 to 0.125
- w_col: bfloat16 [5, 384, 384], replicated, may hold values from -0.125 to 0.125
Outputs:
- hidden: float32 [16, 768, 128], P('band', 'pair'), parts along dimension 1
- flow: float32 [2, 16, 768], P(None, 'band', 'pair'), parts along dimension 2
The draws below stay inside these ranges and needn't reach their ends.
There are 2 independent parts, one for each index of `pair`. The reference program is written for one: setup_inputs(seed, part) draws one part's arguments, and reference() takes and returns one part's arrays. A program takes and returns all parts, laid end to end along the dimension named above; an argument that names none is the same for every part. Nothing has to cross between parts.
Inputs may be any that keep to these rules, and one draw needn't show every extreme that they name: `frame1`: feature vectors. `frame2`: feature vectors. offsets[0] and offsets[1] are each pixel's teacher lookup offsets, in rows and in strips.
All inputs are finite; a program needn't handle non-finite values.
Results may differ from the reference program's by a relative error of at most 0.0041.
Values may be sent and summed in bfloat16 or wider, within the bound.
A program may use at most 64 MiB of HBM per device.

```python
import math
import jax
import jax.numpy as jnp
from jax import lax

C = 256
HID = 128
CTX = 128
MOTION = 128
WIDTH = 384
ITERS = 2
NROWS = 16


def base_field(key, spread):
    return jnp.clip(spread * jax.random.normal(key, (NROWS, WIDTH, C), jnp.float32), -6.0, 6.0)


def displacement(key):
    key_pair = jax.random.split(jax.random.fold_in(key, 3), 2)
    row_move = jax.random.randint(key_pair[0], (), -4, 5).astype(jnp.int32)
    col_move = jax.random.randint(key_pair[1], (), -12, 13).astype(jnp.int32)
    return (row_move, col_move)


def draw_frame1(key, part):
    feature_field = base_field(jax.random.fold_in(key, 1), 1.5)
    return feature_field.astype(jnp.bfloat16)


def draw_frame2(key, part):
    source_field = base_field(jax.random.fold_in(key, 1), 1.5)
    row_move, col_move = displacement(key)
    row_index = ((jnp.arange(NROWS, dtype=jnp.int32) - row_move) % NROWS).astype(jnp.int32)
    col_index = ((jnp.arange(WIDTH, dtype=jnp.int32) - col_move) % WIDTH).astype(jnp.int32)
    moved_field = jnp.take(jnp.take(source_field, row_index, axis=0), col_index, axis=1)
    noise_field = base_field(jax.random.fold_in(key, 2), 0.4)
    feature_field = jnp.clip(moved_field + noise_field, -6.0, 6.0)
    return feature_field.astype(jnp.bfloat16)


def place_ends(entries, own_key, low, top_value):
    longest = entries.shape.index(max(entries.shape))
    spots = []
    for shift in (0, 1):
        where = [jax.random.randint(jax.random.fold_in(own_key, axis), (), 0, length) for axis, length in enumerate(entries.shape)]
        where[longest] = (where[longest] + shift) % entries.shape[longest]
        spots.append(tuple(where))
    return entries.at[spots[0]].set(low).at[spots[1]].set(top_value)


def shard_levels(stream_key, dims, pieces, smallest, high):
    def one(dim, blocks):
        draws = jax.random.uniform(jax.random.fold_in(jax.random.fold_in(stream_key, 6), dim), (blocks,), jnp.float32, smallest / len(pieces), high / len(pieces))
        return jnp.repeat(jnp.exp(draws), dims[dim] // blocks).reshape((-1,) + (1,) * (len(dims) - dim - 1))

    gain = one(*pieces[0])
    for cut in pieces[1:]:
        gain = gain * one(*cut)
    return gain


def noise(key, extent, scale, bound, cuts=(), kind=jnp.bfloat16):
    result = scale * jax.random.normal(key, extent, jnp.float32)
    if cuts:
        result = result * shard_levels(key, extent, cuts, -0.22, 0.18)
    return jnp.clip(result, -bound, bound).astype(kind)


def setup_inputs(seed: int = 0, part: int = 0) -> dict:
    seeds = jax.random.split(jax.random.key(seed), 9)
    own_keys = jax.random.split(jax.random.fold_in(seeds[8], part), 9)
    frame1 = draw_frame1(jax.random.fold_in(jax.random.fold_in(seeds[8], part), 71), part)
    frame2 = draw_frame2(jax.random.fold_in(jax.random.fold_in(seeds[8], part), 71), part)
    context = noise(own_keys[2], (NROWS, WIDTH, CTX), 1.0, 6.0, ((0, 16),))
    hidden_init = jnp.clip(jax.random.uniform(own_keys[3], (NROWS, WIDTH, HID), jnp.float32, -1.0, 1.0) * shard_levels(own_keys[3], (NROWS, WIDTH, HID), ((0, 16),), -0.4, 0.0), -1.0, 1.0).astype(jnp.bfloat16)
    offsets = place_ends(jax.random.randint(own_keys[4], (2, NROWS, WIDTH), -4, 5), jax.random.fold_in(own_keys[4], 1), -4, 4).astype(jnp.int32)
    w_motion = noise(seeds[5], (3, MOTION), 3 ** -0.5, 3.5, (), jnp.float32)
    w_row = noise(seeds[6], (5, HID + CTX + MOTION, 3 * HID), (5 * (HID + CTX + MOTION)) ** -0.5, 0.125)
    w_col = noise(seeds[7], (5, HID + CTX + MOTION, 3 * HID), (5 * (HID + CTX + MOTION)) ** -0.5, 0.125)
    return {"frame1": frame1, "frame2": frame2, "context": context, "hidden_init": hidden_init, "offsets": offsets, "w_motion": w_motion, "w_row": w_row, "w_col": w_col}


def pool_strips(frame2):
    band_rows, image_width, channels = frame2.shape
    blocks = frame2.astype(jnp.float32).reshape(band_rows, image_width // 8, 8, channels)
    return (lax.optimization_barrier(jnp.sum(blocks, axis=2)) / 2.0).astype(jnp.bfloat16)

def lookup_targets(offsets, row_first, total_rows, image_width):
    band_rows = offsets.shape[1]
    pixel_row = row_first + jnp.arange(band_rows, dtype=jnp.int32)[:, None] + jnp.zeros((1, image_width), jnp.int32)
    pixel_col = jnp.zeros((band_rows, 1), jnp.int32) + jnp.arange(image_width, dtype=jnp.int32)[None, :]
    target_row = pixel_row + offsets[0]
    target_col = pixel_col // 8 + offsets[1]
    inside = (target_row >= 0) & (target_row < total_rows) & (target_col >= 0) & (target_col < image_width // 8)
    target_row = jnp.where(inside, target_row, -1).astype(jnp.int32)
    target_col = jnp.where(inside, target_col, -1).astype(jnp.int32)
    return (target_row, target_col, pixel_row, pixel_col)

def strip_step(state, feature_rows, strip_block, row_zero, total_rows, image_width, target_row, target_col):
    block_rows, grid_cols, channels = strip_block.shape
    scores = jnp.dot(feature_rows, strip_block.reshape(block_rows * grid_cols, channels).T, preferred_element_type=jnp.float32) / math.sqrt(channels)
    running_max, denominator, acc_row, acc_col, lookup = state
    new_max = jnp.maximum(running_max, lax.optimization_barrier(jnp.max(scores, axis=1)))
    shrink = jnp.exp(running_max - new_max)
    exponent = jnp.exp(scores - new_max[:, None]).reshape(-1, block_rows, grid_cols)
    strip_row = (row_zero + jnp.arange(block_rows, dtype=jnp.int32)).astype(jnp.int32)
    column_ids = jnp.arange(grid_cols, dtype=jnp.int32)
    row_centre = strip_row.astype(jnp.float32) / total_rows
    col_centre = ((8 * column_ids).astype(jnp.float32) + 3.5) / image_width
    row_weight = lax.optimization_barrier(jnp.sum(exponent, axis=2))
    col_weight = lax.optimization_barrier(jnp.sum(exponent, axis=1))
    scores_grid = scores.reshape(-1, block_rows, grid_cols)
    hit = (strip_row[None, :, None] == target_row[:, None, None]) & (column_ids[None, None, :] == target_col[:, None, None])
    found = lax.optimization_barrier(jnp.sum(jnp.where(hit, scores_grid, 0.0), axis=(1, 2)))
    return (new_max, denominator * shrink + lax.optimization_barrier(jnp.sum(row_weight, axis=1)), acc_row * shrink + lax.optimization_barrier(jnp.sum(row_weight * row_centre[None, :], axis=1)), acc_col * shrink + lax.optimization_barrier(jnp.sum(col_weight * col_centre[None, :], axis=1)), lookup + found)

def conv_valid(source, weight, conv_axis):
    out_count = source.shape[conv_axis] - 4
    summed = None
    for kernel_tap in range(5):
        tap_slice = lax.slice_in_dim(source, kernel_tap, kernel_tap + out_count, axis=conv_axis)
        tap_term = jnp.dot(tap_slice.reshape(-1, tap_slice.shape[-1]), weight[kernel_tap], preferred_element_type=jnp.float32)
        summed = tap_term if summed is None else summed + tap_term
    out_shape = tuple(tap_slice.shape[:-1]) + (weight.shape[-1],)
    return summed.reshape(out_shape)

def conv_padded(source, weight, conv_axis):
    widths = [(0, 0), (0, 0), (0, 0)]
    widths[conv_axis] = (2, 2)
    return conv_valid(jnp.pad(source, widths), weight, conv_axis)

def gru_pass(hidden, inputs, weight, conv_axis):
    width_h = hidden.shape[-1]
    from_inputs = conv_padded(inputs, weight[:, width_h:, :], conv_axis)
    hidden_half = lax.optimization_barrier(hidden.astype(jnp.bfloat16))
    gate_pair = jax.nn.sigmoid(conv_padded(hidden_half, weight[:, :width_h, :2 * width_h], conv_axis) + from_inputs[..., :2 * width_h])
    update_gate = gate_pair[..., :width_h]
    reset_gate = gate_pair[..., width_h:]
    gated = (reset_gate * hidden_half.astype(jnp.float32)).astype(jnp.bfloat16)
    candidate = jnp.tanh(conv_padded(gated, weight[:, :width_h, 2 * width_h:], conv_axis) + from_inputs[..., 2 * width_h:])
    return (1.0 - update_gate) * hidden + update_gate * candidate

def reference(frame1, frame2, context, hidden_init, offsets, w_motion, w_row, w_col):
    strips = pool_strips(frame2)
    target_row, target_col, pixel_row, pixel_col = lookup_targets(offsets, jnp.zeros((), jnp.int32), NROWS, WIDTH)

    def match_row(args):
        feature_rows, rows_target, cols_target = args
        begin = jnp.full((WIDTH,), -jnp.inf, jnp.float32)
        empty = jnp.zeros((WIDTH,), jnp.float32)
        state = (begin, empty, empty, empty, empty)
        final = strip_step(state, feature_rows, strips, jnp.zeros((), jnp.int32), NROWS, WIDTH, rows_target, cols_target)
        return (final[2] / final[1], final[3] / final[1], final[4])
    moved_row, moved_col, lookup = lax.map(match_row, (frame1, target_row, target_col))
    flow_row = moved_row - pixel_row.astype(jnp.float32) / NROWS
    flow_col = moved_col - pixel_col.astype(jnp.float32) / WIDTH
    motion = jax.nn.relu(flow_row[..., None] * w_motion[0] + flow_col[..., None] * w_motion[1] + lookup[..., None] * w_motion[2]).astype(jnp.bfloat16)
    inputs = jnp.concatenate([context, motion], axis=-1)
    hidden = hidden_init.astype(jnp.float32)
    for iteration in range(ITERS):
        hidden = gru_pass(hidden, inputs, w_row, 1)
        hidden = gru_pass(hidden, inputs, w_col, 0)
    return (hidden, jnp.stack([flow_row, flow_col]))
```

```python
import functools
import math

import jax
import jax.numpy as jnp
from jax import lax
from jax.experimental import pallas as pl
from jax.experimental.pallas import tpu as pltpu
from jax.sharding import PartitionSpec as P

ITERS = 2


def passed_along(array, axis, by):
    count = lax.axis_size(axis)
    pairs = [(i, i + by) for i in range(count) if 0 <= i + by < count]
    return lax.ppermute(array, axis, pairs)


def pool_strips(frame2):
    band_rows, image_width, channels = frame2.shape
    blocks = frame2.astype(jnp.float32).reshape(band_rows, image_width // 8, 8, channels)
    return (jnp.sum(blocks, axis=2) / 2.0).astype(jnp.bfloat16)


def lookup_targets(offsets, row_first, total_rows, image_width):
    band_rows = offsets.shape[1]
    pixel_row = (
        row_first
        + jnp.arange(band_rows, dtype=jnp.int32)[:, None]
        + jnp.zeros((1, image_width), jnp.int32)
    )
    pixel_col = jnp.arange(image_width, dtype=jnp.int32)[None, :]
    target_row = pixel_row + offsets[0]
    target_col = pixel_col // 8 + offsets[1]
    inside = (
        (target_row >= 0)
        & (target_row < total_rows)
        & (target_col >= 0)
        & (target_col < image_width // 8)
    )
    target_row = jnp.where(inside, target_row, -1)
    target_col = jnp.where(inside, target_col, -1)
    return (target_row, target_col, pixel_row, pixel_col)


def strip_step(
    state, feature_rows, strip_block, row_zero, total_rows, image_width, target_row, target_col
):
    block_rows, grid_cols, channels = strip_block.shape
    scores = jnp.dot(
        feature_rows,
        strip_block.reshape(block_rows * grid_cols, channels).T,
        preferred_element_type=jnp.float32,
    ) / math.sqrt(channels)
    running_max, denominator, acc_row, acc_col, lookup = state
    new_max = jnp.maximum(running_max, jnp.max(scores, axis=1))
    shrink = jnp.exp(running_max - new_max)
    exponent = jnp.exp(scores - new_max[:, None]).reshape(-1, block_rows, grid_cols)
    strip_row = row_zero + jnp.arange(block_rows, dtype=jnp.int32)
    column_ids = jnp.arange(grid_cols, dtype=jnp.int32)
    row_centre = strip_row.astype(jnp.float32) / total_rows
    col_centre = ((8 * column_ids).astype(jnp.float32) + 3.5) / image_width
    row_weight = jnp.sum(exponent, axis=2)
    col_weight = jnp.sum(exponent, axis=1)
    scores_grid = scores.reshape(-1, block_rows, grid_cols)
    hit = (strip_row[None, :, None] == target_row[:, None, None]) & (
        column_ids[None, None, :] == target_col[:, None, None]
    )
    found = jnp.sum(jnp.where(hit, scores_grid, 0.0), axis=(1, 2))
    return (
        new_max,
        denominator * shrink + jnp.sum(row_weight, axis=1),
        acc_row * shrink + jnp.sum(row_weight * row_centre[None, :], axis=1),
        acc_col * shrink + jnp.sum(col_weight * col_centre[None, :], axis=1),
        lookup + found,
    )


def conv_valid(source, weight, conv_axis):
    out_count = source.shape[conv_axis] - 4
    summed = None
    for kernel_tap in range(5):
        tap_slice = lax.slice_in_dim(source, kernel_tap, kernel_tap + out_count, axis=conv_axis)
        tap_term = jnp.dot(
            tap_slice.reshape(-1, tap_slice.shape[-1]),
            weight[kernel_tap],
            preferred_element_type=jnp.float32,
        )
        summed = tap_term if summed is None else summed + tap_term
    out_shape = tuple(tap_slice.shape[:-1]) + (weight.shape[-1],)
    return summed.reshape(out_shape)


def pad_columns(source):
    return jnp.pad(source, ((0, 0), (2, 2), (0, 0)))


def rows_around(source, depth, mover):
    above = [
        mover(source, offset)
        for offset in list(range(depth, 0, -1)) + list(range(-1, -depth - 1, -1))
    ]
    return jnp.concatenate(above[:depth] + [source] + above[depth:], axis=0)


def row_pass(hidden, from_inputs, weight):
    width_h = hidden.shape[-1]
    hidden_half = lax.optimization_barrier(hidden.astype(jnp.bfloat16))
    gate_pair = jax.nn.sigmoid(
        conv_valid(pad_columns(hidden_half), weight[:, :width_h, : 2 * width_h], 1)
        + from_inputs[..., : 2 * width_h]
    )
    update_gate = gate_pair[..., :width_h]
    reset_gate = gate_pair[..., width_h:]
    gated = (reset_gate * hidden_half.astype(jnp.float32)).astype(jnp.bfloat16)
    candidate = jnp.tanh(
        conv_valid(pad_columns(gated), weight[:, :width_h, 2 * width_h :], 1)
        + from_inputs[..., 2 * width_h :]
    )
    return (1.0 - update_gate) * hidden + update_gate * candidate


def column_pass_each(hidden, from_inputs, weight):
    width_h = hidden.shape[-1]
    hidden_half = lax.optimization_barrier(hidden.astype(jnp.bfloat16))
    hidden_ext = rows_around(
        hidden_half, 2, lambda source, offset: passed_along(source, "band", offset)
    )
    gate_pair = jax.nn.sigmoid(
        conv_valid(hidden_ext, weight[:, :width_h, : 2 * width_h], 0)
        + from_inputs[..., : 2 * width_h]
    )
    update_gate = gate_pair[..., :width_h]
    reset_gate = gate_pair[..., width_h:]
    gated = (reset_gate * hidden_half.astype(jnp.float32)).astype(jnp.bfloat16)
    gated_ext = rows_around(gated, 2, lambda source, offset: passed_along(source, "band", offset))
    candidate = jnp.tanh(
        conv_valid(gated_ext, weight[:, :width_h, 2 * width_h :], 0)
        + from_inputs[..., 2 * width_h :]
    )
    return (1.0 - update_gate) * hidden + update_gate * candidate


def per_device_rows(frame1, frame2, context, hidden_init, offsets, w_motion, w_row, w_col):
    band_rows, image_width, channels = frame1.shape
    total_rows = band_rows * lax.axis_size("band")
    row_first = lax.axis_index("band") * band_rows
    strips = pool_strips(frame2)
    target_row, target_col, pixel_row, pixel_col = lookup_targets(
        offsets, row_first, total_rows, image_width
    )
    pixel_count = band_rows * image_width
    features = frame1.reshape(pixel_count, channels)
    rows_target = target_row.reshape(pixel_count)
    cols_target = target_col.reshape(pixel_count)
    zeros_state = jnp.zeros((pixel_count,), jnp.float32)
    initial = (
        jnp.full((pixel_count,), -jnp.inf, jnp.float32),
        zeros_state,
        zeros_state,
        zeros_state,
        zeros_state,
    )
    state = initial
    arriving = lax.all_gather(strips, "band", axis=0, tiled=True)
    arriving_rows = arriving.shape[0]
    step_rows = min(arriving_rows, 16)
    full_steps = arriving_rows // step_rows
    blocks = arriving.reshape((full_steps, step_rows) + arriving.shape[1:])
    starts = step_rows * jnp.arange(full_steps, dtype=jnp.int32)

    def advance(carry, pieces):
        return (
            strip_step(
                carry,
                features,
                pieces[0],
                pieces[1],
                total_rows,
                image_width,
                rows_target,
                cols_target,
            ),
            None,
        )

    state, unused = lax.scan(advance, state, (blocks, starts))
    running_max, denominator, acc_row, acc_col, lookup = state
    flow_row = (acc_row / denominator).reshape(band_rows, image_width) - pixel_row.astype(
        jnp.float32
    ) / total_rows
    flow_col = (acc_col / denominator).reshape(band_rows, image_width) - pixel_col.astype(
        jnp.float32
    ) / image_width
    lookup = lookup.reshape(band_rows, image_width)
    motion = jax.nn.relu(
        flow_row[..., None] * w_motion[0]
        + flow_col[..., None] * w_motion[1]
        + lookup[..., None] * w_motion[2]
    ).astype(jnp.bfloat16)
    inputs = jnp.concatenate([context, motion], axis=-1)
    width_h = hidden_init.shape[-1]
    from_row = conv_valid(pad_columns(inputs), w_row[:, width_h:, :], 1)
    hidden = hidden_init.astype(jnp.float32)
    inputs_ext = rows_around(inputs, 2, lambda source, offset: passed_along(source, "band", offset))
    from_col = conv_valid(inputs_ext, w_col[:, width_h:, :], 0)
    for iteration in range(ITERS):
        hidden = row_pass(hidden, from_row, w_row)
        hidden = column_pass_each(hidden, from_col, w_col)
    return (hidden, jnp.stack([flow_row, flow_col]))


BF = jnp.bfloat16
F32 = jnp.float32
MESH = pl.DeviceIdType.MESH
HALO = 4


def mm(a, b):
    return jnp.dot(a, b, preferred_element_type=F32)


def shifted_taps(padded, count):
    return jnp.concatenate(
        [padded[6 + k : 6 + k + count, :].astype(BF) for k in range(5)], axis=1
    )


def row_taps(value, step):
    zeros = jnp.zeros((2 * step, value.shape[1]), value.dtype)
    tall = jnp.concatenate([zeros, value, zeros], axis=0)
    count = value.shape[0]
    return jnp.concatenate([tall[k * step : k * step + count] for k in range(5)], axis=1)


def tap_weights(w_ref, first, low, high):
    return w_ref[:, first : first + 128, low:high].reshape(5 * 128, high - low)


def fused_kernel(
    bands,
    frame1,
    frame2,
    context,
    hidden_init,
    offsets,
    w_motion,
    w_row_hbm,
    w_col_hbm,
    hidden_out,
    flow_out,
    w_row,
    w_col,
    strips,
    scores,
    ctx_stage,
    ctx_recv,
    flow_stage,
    flow_recv,
    hid_stage,
    hid_recv,
    out_stage,
    out_recv,
    pad_ctx,
    pad_hid,
    pad_mot,
    pad_gate,
    win_ctx,
    win_mot,
    win_hid,
    win_gate,
    acc_row,
    gate_row,
    acc_col,
    acc_row2,
    w_sem,
    strip_send,
    strip_recv,
    ctx_ssem,
    ctx_rsem,
    flow_ssem,
    flow_rsem,
    hid_ssem,
    hid_rsem,
    out_ssem,
    out_rsem,
):
    width = frame1.shape[0]
    own = width // bands
    win = own + 2 * HALO
    grid_cols = width // 8
    me = lax.axis_index("band")
    pair = lax.axis_index("pair")

    copy_row = pltpu.make_async_copy(w_row_hbm, w_row, w_sem.at[0])
    copy_col = pltpu.make_async_copy(w_col_hbm, w_col, w_sem.at[1])
    copy_row.start()
    copy_col.start()

    barrier = pltpu.get_barrier_semaphore()

    def greet(k, carry):
        pl.semaphore_signal(
            barrier, inc=1, device_id=(lax.rem(me + k, bands), pair), device_id_type=MESH
        )
        return carry

    lax.fori_loop(1, bands, greet, 0)

    blocks = frame2[...].astype(F32).reshape(grid_cols, 8, frame2.shape[1])
    strips[pl.ds(me, 1)] = (jnp.sum(blocks, axis=1) / 2.0).astype(BF)[None]

    def zero_ends(ref, count):
        ref[0:8, :] = jnp.zeros((8, 128), F32)
        ref[8 + count : 16 + count, :] = jnp.zeros((8, 128), F32)

    for ref in (pad_ctx, pad_hid, pad_mot, pad_gate):
        zero_ends(ref, width)
    for ref in (win_ctx, win_mot, win_hid, win_gate):
        zero_ends(ref, bands * win)

    pad_ctx[8 : 8 + width, :] = context[...].astype(F32)
    pad_hid[8 : 8 + width, :] = hidden_init[...].astype(F32)

    def stage_windows(stage, padded):
        for d in range(bands):
            first = 8 + own * d - HALO
            stage[d] = padded[first : first + win, :].astype(BF)

    stage_windows(ctx_stage, pad_ctx)

    def send(stage, recv, ssem, rsem, to):
        return pltpu.make_async_remote_copy(
            src_ref=stage.at[to],
            dst_ref=recv.at[me],
            send_sem=ssem.at[to],
            recv_sem=rsem.at[me],
            device_id=(to, pair),
            device_id_type=MESH,
        )

    def scatter(stage, recv, ssem, rsem):
        def one(k, carry):
            send(stage, recv, ssem, rsem, lax.rem(me + k, bands)).start()
            return carry

        lax.fori_loop(1, bands, one, 0)
        recv[pl.ds(me, 1)] = stage[pl.ds(me, 1)]

    def collect(stage, recv, ssem, rsem):
        def one(k, carry):
            source = lax.rem(me + bands - k, bands)
            pltpu.make_async_remote_copy(
                src_ref=stage.at[source],
                dst_ref=recv.at[source],
                send_sem=ssem.at[source],
                recv_sem=rsem.at[source],
                device_id=(source, pair),
                device_id_type=MESH,
            ).wait_recv()
            return carry

        lax.fori_loop(1, bands, one, 0)

    def sent(stage, recv, ssem, rsem):
        def one(k, carry):
            send(stage, recv, ssem, rsem, lax.rem(me + k, bands)).wait_send()
            return carry

        lax.fori_loop(1, bands, one, 0)

    pl.semaphore_wait(barrier, bands - 1)

    level = me // 4
    place = lax.rem(me, 4)
    core = lax.rem(me, 2)
    sibling = me + 1 - 2 * core
    across = me + 2 - 4 * lax.rem(me // 2, 2)
    levels = (
        level,
        level + 1 - 2 * lax.rem(level, 2),
        2 - level // 2,
        3 - 3 * (level // 2),
    )
    line = [4 * other + place for other in levels]
    across_line = [4 * other + (across - 4 * level) for other in levels]
    started = []

    def pass_on(block, to, slot):
        copy = pltpu.make_async_remote_copy(
            src_ref=strips.at[block],
            dst_ref=strips.at[block],
            send_sem=strip_send.at[slot],
            recv_sem=strip_recv.at[block],
            device_id=(to, pair),
            device_id_type=MESH,
        )
        copy.start()
        started.append(copy)

    def arrived(block):
        pltpu.make_async_remote_copy(
            src_ref=strips.at[block],
            dst_ref=strips.at[block],
            send_sem=strip_send.at[0],
            recv_sem=strip_recv.at[block],
            device_id=(sibling, pair),
            device_id_type=MESH,
        ).wait_recv()

    pass_on(me, line[1], 0)
    pass_on(me, across, 1)
    pass_on(me, line[2], 2)
    pass_on(me, line[3], 3)
    pass_on(me, sibling, 4)

    copy_row.wait()
    gate_row[...] = mm(shifted_taps(pad_hid, width), tap_weights(w_row, 0, 0, 256))

    for i in (1, 2, 3):
        arrived(line[i])
        pass_on(line[i], across, 4 + i)
        pass_on(line[i], sibling, 7 + i)
    scatter(ctx_stage, ctx_recv, ctx_ssem, ctx_rsem)
    acc_row[...] = mm(shifted_taps(pad_ctx, width), tap_weights(w_row, 128, 0, 384))
    for i in (0, 1, 2, 3):
        arrived(across_line[i])
        pass_on(across_line[i], sibling, 11 + i)
    for i in (0, 1, 2, 3):
        arrived(line[i] + 1 - 2 * core)
    for i in (0, 1, 2, 3):
        arrived(across_line[i] + 1 - 2 * core)

    scores[...] = lax.dot_general(
        strips[...].reshape(bands * grid_cols, frame1.shape[1]),
        frame1[...],
        (((1,), (1,)), ((), ())),
        preferred_element_type=F32,
    ) * (1.0 / math.sqrt(frame1.shape[1]))

    row_f = me.astype(F32) / bands
    parts = []
    strip_ids = lax.broadcasted_iota(jnp.int32, (grid_cols, 128), 0)
    centres = ((8 * strip_ids).astype(F32) + 3.5) / width
    for lanes in range(0, width, 128):
        cut = slice(lanes, lanes + 128)
        column = lanes + lax.broadcasted_iota(jnp.int32, (1, 128), 1)
        target_row = me + offsets[0, :, cut]
        target_col = column // 8 + offsets[1, :, cut]
        inside = (
            (target_row >= 0)
            & (target_row < bands)
            & (target_col >= 0)
            & (target_col < grid_cols)
        )
        target = jnp.where(inside, target_row * grid_cols + target_col, -1)
        highest = scores[0:grid_cols, cut]
        for r in range(1, bands):
            highest = jnp.maximum(highest, scores[r * grid_cols : (r + 1) * grid_cols, cut])
        highest = jnp.max(highest, axis=0, keepdims=True)
        by_col = jnp.zeros((grid_cols, 128), F32)
        by_row = jnp.zeros((8, 128), F32)
        found = jnp.zeros((grid_cols, 128), F32)
        for r in range(bands):
            block = scores[r * grid_cols : (r + 1) * grid_cols, cut]
            raised = jnp.exp(block - highest)
            by_col = by_col + raised
            if r:
                folded = jnp.sum(raised.reshape(grid_cols // 8, 8, 128), axis=0)
                by_row = by_row + folded * (r / bands)
            found = found + jnp.where(strip_ids + r * grid_cols == target, block, 0.0)
        total = jnp.sum(by_col, axis=0, keepdims=True)
        moved_row = jnp.sum(by_row, axis=0, keepdims=True) / total
        moved_col = jnp.sum(by_col * centres, axis=0, keepdims=True) / total
        flow_row = moved_row - row_f
        flow_col = moved_col - column.astype(F32) / width
        flow_out[0, :, cut] = flow_row
        flow_out[1, :, cut] = flow_col
        parts.append(
            jnp.concatenate(
                [
                    flow_row,
                    flow_col,
                    jnp.sum(found, axis=0, keepdims=True),
                    jnp.zeros((5, 128), F32),
                ],
                axis=0,
            )
        )

    three = jnp.concatenate(parts + [jnp.zeros((8, 128), F32)], axis=1)
    span = width + 128
    line_id = lax.broadcasted_iota(jnp.int32, (8, span), 0)
    spread = jnp.where(line_id == 1, pltpu.roll(three, 32, 1), three)
    spread = jnp.where(line_id == 2, pltpu.roll(three, 64, 1), spread)
    lane_group = lax.broadcasted_iota(jnp.int32, (8, 128), 1) // 32
    wanted = lane_group == lax.broadcasted_iota(jnp.int32, (8, 128), 0)
    for d in range(bands):
        turned = pltpu.roll(spread, (span - (own * d - HALO)) % span, 1)[:, 0:128]
        flow_stage[d] = jnp.sum(jnp.where(wanted, turned, 0.0), axis=0, keepdims=True)
    scatter(flow_stage, flow_recv, flow_ssem, flow_rsem)

    def motion_of(first, second, third):
        return jnp.maximum(
            first * w_motion[0:1, :] + second * w_motion[1:2, :] + third * w_motion[2:3, :],
            0.0,
        )

    for i, part in enumerate(parts):
        upright = jnp.concatenate([part, jnp.zeros((120, 128), F32)], axis=0).T
        pad_mot[8 + 128 * i : 136 + 128 * i, :] = motion_of(
            upright[:, 0:1], upright[:, 1:2], upright[:, 2:3]
        )
    acc = mm(shifted_taps(pad_mot, width), tap_weights(w_row, 256, 0, 384)) + acc_row[...]
    start = pad_hid[8 : 8 + width, :]
    update = jax.nn.sigmoid(gate_row[:, 0:128] + acc[:, 0:128])
    reset = jax.nn.sigmoid(gate_row[:, 128:256] + acc[:, 128:256])
    pad_gate[8 : 8 + width, :] = reset * start
    candidate = jnp.tanh(
        mm(shifted_taps(pad_gate, width), tap_weights(w_row, 0, 256, 384)) + acc[:, 256:384]
    )
    pad_hid[8 : 8 + width, :] = (1.0 - update) * start + update * candidate
    stage_windows(hid_stage, pad_hid)
    scatter(hid_stage, hid_recv, hid_ssem, hid_rsem)

    pixels = bands * win
    collect(ctx_stage, ctx_recv, ctx_ssem, ctx_rsem)
    copy_col.wait()
    ctx = ctx_recv[...].reshape(pixels, 128)
    win_ctx[8 : 8 + pixels, :] = ctx.astype(F32)
    acc_col[...] = mm(row_taps(ctx, win), tap_weights(w_col, 128, 0, 384))
    acc_row2[...] = mm(shifted_taps(win_ctx, pixels), tap_weights(w_row, 128, 0, 384))
    collect(flow_stage, flow_recv, flow_ssem, flow_rsem)
    upright = jnp.concatenate(
        [flow_recv[r] for r in range(bands)] + [jnp.zeros((128 - bands, 128), F32)], axis=0
    ).T
    for r in range(bands):
        win_mot[8 + win * r : 8 + win * (r + 1), :] = motion_of(
            upright[0:win, r : r + 1],
            upright[win : 2 * win, r : r + 1],
            upright[2 * win : 3 * win, r : r + 1],
        )
    motion = win_mot[8 : 8 + pixels, :].astype(BF)
    acc_col[...] += mm(row_taps(motion, win), tap_weights(w_col, 256, 0, 384))
    acc_row2[...] += mm(shifted_taps(win_mot, pixels), tap_weights(w_row, 256, 0, 384))

    collect(hid_stage, hid_recv, hid_ssem, hid_rsem)
    state_half = hid_recv[...].reshape(pixels, 128)
    state = state_half.astype(F32)

    def gru(state, half, acc, weight, taps_of):
        pre = mm(taps_of(half, win_hid), tap_weights(weight, 0, 0, 256)) + acc[:, 0:256]
        update = jax.nn.sigmoid(pre[:, 0:128])
        reset = jax.nn.sigmoid(pre[:, 128:256])
        gated = (reset * half.astype(F32)).astype(BF)
        candidate = jnp.tanh(
            mm(taps_of(gated, win_gate), tap_weights(weight, 0, 256, 384)) + acc[:, 256:384]
        )
        return (1.0 - update) * state + update * candidate

    def taps_down(value, unused):
        return row_taps(value, win)

    def taps_along(value, padded):
        padded[8 : 8 + pixels, :] = value.astype(F32)
        return shifted_taps(padded, pixels)

    state = gru(state, state_half, acc_col, w_col, taps_down)
    state = gru(state, state.astype(BF), acc_row2, w_row, taps_along)
    state = gru(state, state.astype(BF), acc_col, w_col, taps_down)
    win_hid[8 : 8 + pixels, :] = state
    for r in range(bands):
        first = 8 + win * r + HALO
        out_stage[r] = win_hid[first : first + own, :].astype(BF)
    scatter(out_stage, out_recv, out_ssem, out_rsem)
    for copy in started:
        copy.wait_send()
    sent(ctx_stage, ctx_recv, ctx_ssem, ctx_rsem)
    sent(flow_stage, flow_recv, flow_ssem, flow_rsem)
    sent(hid_stage, hid_recv, hid_ssem, hid_rsem)
    collect(out_stage, out_recv, out_ssem, out_rsem)
    hidden_out[...] = out_recv[...]
    sent(out_stage, out_recv, out_ssem, out_rsem)


def per_device_columns(
    bands, frame1, frame2, context, hidden_init, offsets, w_motion, w_row, w_col
):
    unused, width, channels = frame1.shape
    own = width // bands
    win = own + 2 * HALO
    pixels = bands * win
    vmem = pl.BlockSpec(memory_space=pltpu.VMEM)
    hbm = pl.BlockSpec(memory_space=pl.ANY)
    dma = pltpu.SemaphoreType.DMA
    tall = pltpu.VMEM((width + 16, 128), F32)
    wide = pltpu.VMEM((pixels + 16, 128), F32)
    hidden, flow = pl.pallas_call(
        functools.partial(fused_kernel, bands),
        out_shape=(
            jax.ShapeDtypeStruct((bands, own, 128), BF),
            jax.ShapeDtypeStruct((2, 1, width), F32),
        ),
        in_specs=[vmem] * 6 + [hbm] * 2,
        out_specs=(vmem, vmem),
        scratch_shapes=[
            pltpu.VMEM(w_row.shape, BF),
            pltpu.VMEM(w_col.shape, BF),
            pltpu.VMEM((bands, width // 8, channels), BF),
            pltpu.VMEM((bands * width // 8, width), F32),
            pltpu.VMEM((bands, win, 128), BF),
            pltpu.VMEM((bands, win, 128), BF),
            pltpu.VMEM((bands, 1, 128), F32),
            pltpu.VMEM((bands, 1, 128), F32),
            pltpu.VMEM((bands, win, 128), BF),
            pltpu.VMEM((bands, win, 128), BF),
            pltpu.VMEM((bands, own, 128), BF),
            pltpu.VMEM((bands, own, 128), BF),
            tall,
            tall,
            tall,
            tall,
            wide,
            wide,
            wide,
            wide,
            pltpu.VMEM((width, 384), F32),
            pltpu.VMEM((width, 256), F32),
            pltpu.VMEM((pixels, 384), F32),
            pltpu.VMEM((pixels, 384), F32),
            dma((2,)),
            dma((15,)),
        ]
        + [dma((bands,))] * 9,
        compiler_params=pltpu.CompilerParams(
            collective_id=0, has_side_effects=True, vmem_limit_bytes=48 * 1024 * 1024
        ),
        cost_estimate=pl.CostEstimate(
            flops=2_400_000_000, bytes_accessed=4_500_000, transcendentals=700_000
        ),
    )(
        frame1.reshape(width, channels),
        frame2.reshape(width, channels),
        context.reshape(width, 128),
        hidden_init.reshape(width, 128),
        offsets,
        w_motion,
        w_row,
        w_col,
    )
    return (hidden.astype(F32).reshape(1, width, 128), flow)


def solution(mesh):
    bands = mesh.shape["band"]

    def per_device(frame1, frame2, *rest):
        own = frame1.shape[1] // bands
        if bands == 16 and frame1.shape[0] == 1 and own + 2 * HALO == 32:
            return per_device_columns(bands, frame1, frame2, *rest)
        return per_device_rows(frame1, frame2, *rest)

    return jax.shard_map(
        per_device,
        mesh=mesh,
        in_specs=(
            P("band", "pair", None),
            P("band", "pair", None),
            P("band", "pair", None),
            P("band", "pair", None),
            P(None, "band", "pair"),
            P(),
            P(),
            P(),
        ),
        out_specs=(P("band", "pair", None), P(None, "band", "pair")),
        check_vma=False,
    )
```

```python
import functools
import math

import jax
import jax.numpy as jnp
from jax import lax
from jax.experimental import pallas as pl
from jax.experimental.pallas import tpu as pltpu
from jax.sharding import PartitionSpec as P

ITERS = 2


def passed_along(array, axis, by):
    count = lax.axis_size(axis)
    pairs = [(i, i + by) for i in range(count) if 0 <= i + by < count]
    return lax.ppermute(array, axis, pairs)


def pool_strips(frame2):
    band_rows, image_width, channels = frame2.shape
    blocks = frame2.astype(jnp.float32).reshape(band_rows, image_width // 8, 8, channels)
    return (jnp.sum(blocks, axis=2) / 2.0).astype(jnp.bfloat16)


def lookup_targets(offsets, row_first, total_rows, image_width):
    band_rows = offsets.shape[1]
    pixel_row = (
        row_first
        + jnp.arange(band_rows, dtype=jnp.int32)[:, None]
        + jnp.zeros((1, image_width), jnp.int32)
    )
    pixel_col = jnp.arange(image_width, dtype=jnp.int32)[None, :]
    target_row = pixel_row + offsets[0]
    target_col = pixel_col // 8 + offsets[1]
    inside = (
        (target_row >= 0)
        & (target_row < total_rows)
        & (target_col >= 0)
        & (target_col < image_width // 8)
    )
    target_row = jnp.where(inside, target_row, -1)
    target_col = jnp.where(inside, target_col, -1)
    return (target_row, target_col, pixel_row, pixel_col)


def strip_step(
    state, feature_rows, strip_block, row_zero, total_rows, image_width, target_row, target_col
):
    block_rows, grid_cols, channels = strip_block.shape
    scores = jnp.dot(
        feature_rows,
        strip_block.reshape(block_rows * grid_cols, channels).T,
        preferred_element_type=jnp.float32,
    ) / math.sqrt(channels)
    running_max, denominator, acc_row, acc_col, lookup = state
    new_max = jnp.maximum(running_max, jnp.max(scores, axis=1))
    shrink = jnp.exp(running_max - new_max)
    exponent = jnp.exp(scores - new_max[:, None]).reshape(-1, block_rows, grid_cols)
    strip_row = row_zero + jnp.arange(block_rows, dtype=jnp.int32)
    column_ids = jnp.arange(grid_cols, dtype=jnp.int32)
    row_centre = strip_row.astype(jnp.float32) / total_rows
    col_centre = ((8 * column_ids).astype(jnp.float32) + 3.5) / image_width
    row_weight = jnp.sum(exponent, axis=2)
    col_weight = jnp.sum(exponent, axis=1)
    scores_grid = scores.reshape(-1, block_rows, grid_cols)
    hit = (strip_row[None, :, None] == target_row[:, None, None]) & (
        column_ids[None, None, :] == target_col[:, None, None]
    )
    found = jnp.sum(jnp.where(hit, scores_grid, 0.0), axis=(1, 2))
    return (
        new_max,
        denominator * shrink + jnp.sum(row_weight, axis=1),
        acc_row * shrink + jnp.sum(row_weight * row_centre[None, :], axis=1),
        acc_col * shrink + jnp.sum(col_weight * col_centre[None, :], axis=1),
        lookup + found,
    )


def conv_valid(source, weight, conv_axis):
    out_count = source.shape[conv_axis] - 4
    summed = None
    for kernel_tap in range(5):
        tap_slice = lax.slice_in_dim(source, kernel_tap, kernel_tap + out_count, axis=conv_axis)
        tap_term = jnp.dot(
            tap_slice.reshape(-1, tap_slice.shape[-1]),
            weight[kernel_tap],
            preferred_element_type=jnp.float32,
        )
        summed = tap_term if summed is None else summed + tap_term
    out_shape = tuple(tap_slice.shape[:-1]) + (weight.shape[-1],)
    return summed.reshape(out_shape)


def pad_columns(source):
    return jnp.pad(source, ((0, 0), (2, 2), (0, 0)))


def rows_around(source, depth, mover):
    above = [
        mover(source, offset)
        for offset in list(range(depth, 0, -1)) + list(range(-1, -depth - 1, -1))
    ]
    return jnp.concatenate(above[:depth] + [source] + above[depth:], axis=0)


def row_pass(hidden, from_inputs, weight):
    width_h = hidden.shape[-1]
    hidden_half = lax.optimization_barrier(hidden.astype(jnp.bfloat16))
    gate_pair = jax.nn.sigmoid(
        conv_valid(pad_columns(hidden_half), weight[:, :width_h, : 2 * width_h], 1)
        + from_inputs[..., : 2 * width_h]
    )
    update_gate = gate_pair[..., :width_h]
    reset_gate = gate_pair[..., width_h:]
    gated = (reset_gate * hidden_half.astype(jnp.float32)).astype(jnp.bfloat16)
    candidate = jnp.tanh(
        conv_valid(pad_columns(gated), weight[:, :width_h, 2 * width_h :], 1)
        + from_inputs[..., 2 * width_h :]
    )
    return (1.0 - update_gate) * hidden + update_gate * candidate


def column_pass_each(hidden, from_inputs, weight):
    width_h = hidden.shape[-1]
    hidden_half = lax.optimization_barrier(hidden.astype(jnp.bfloat16))
    hidden_ext = rows_around(
        hidden_half, 2, lambda source, offset: passed_along(source, "band", offset)
    )
    gate_pair = jax.nn.sigmoid(
        conv_valid(hidden_ext, weight[:, :width_h, : 2 * width_h], 0)
        + from_inputs[..., : 2 * width_h]
    )
    update_gate = gate_pair[..., :width_h]
    reset_gate = gate_pair[..., width_h:]
    gated = (reset_gate * hidden_half.astype(jnp.float32)).astype(jnp.bfloat16)
    gated_ext = rows_around(gated, 2, lambda source, offset: passed_along(source, "band", offset))
    candidate = jnp.tanh(
        conv_valid(gated_ext, weight[:, :width_h, 2 * width_h :], 0)
        + from_inputs[..., 2 * width_h :]
    )
    return (1.0 - update_gate) * hidden + update_gate * candidate


def per_device_rows(frame1, frame2, context, hidden_init, offsets, w_motion, w_row, w_col):
    band_rows, image_width, channels = frame1.shape
    total_rows = band_rows * lax.axis_size("band")
    row_first = lax.axis_index("band") * band_rows
    strips = pool_strips(frame2)
    target_row, target_col, pixel_row, pixel_col = lookup_targets(
        offsets, row_first, total_rows, image_width
    )
    pixel_count = band_rows * image_width
    features = frame1.reshape(pixel_count, channels)
    rows_target = target_row.reshape(pixel_count)
    cols_target = target_col.reshape(pixel_count)
    zeros_state = jnp.zeros((pixel_count,), jnp.float32)
    initial = (
        jnp.full((pixel_count,), -jnp.inf, jnp.float32),
        zeros_state,
        zeros_state,
        zeros_state,
        zeros_state,
    )
    state = initial
    arriving = lax.all_gather(strips, "band", axis=0, tiled=True)
    arriving_rows = arriving.shape[0]
    step_rows = min(arriving_rows, 16)
    full_steps = arriving_rows // step_rows
    blocks = arriving.reshape((full_steps, step_rows) + arriving.shape[1:])
    starts = step_rows * jnp.arange(full_steps, dtype=jnp.int32)

    def advance(carry, pieces):
        return (
            strip_step(
                carry,
                features,
                pieces[0],
                pieces[1],
                total_rows,
                image_width,
                rows_target,
                cols_target,
            ),
            None,
        )

    state, unused = lax.scan(advance, state, (blocks, starts))
    running_max, denominator, acc_row, acc_col, lookup = state
    flow_row = (acc_row / denominator).reshape(band_rows, image_width) - pixel_row.astype(
        jnp.float32
    ) / total_rows
    flow_col = (acc_col / denominator).reshape(band_rows, image_width) - pixel_col.astype(
        jnp.float32
    ) / image_width
    lookup = lookup.reshape(band_rows, image_width)
    motion = jax.nn.relu(
        flow_row[..., None] * w_motion[0]
        + flow_col[..., None] * w_motion[1]
        + lookup[..., None] * w_motion[2]
    ).astype(jnp.bfloat16)
    inputs = jnp.concatenate([context, motion], axis=-1)
    width_h = hidden_init.shape[-1]
    from_row = conv_valid(pad_columns(inputs), w_row[:, width_h:, :], 1)
    hidden = hidden_init.astype(jnp.float32)
    inputs_ext = rows_around(inputs, 2, lambda source, offset: passed_along(source, "band", offset))
    from_col = conv_valid(inputs_ext, w_col[:, width_h:, :], 0)
    for iteration in range(ITERS):
        hidden = row_pass(hidden, from_row, w_row)
        hidden = column_pass_each(hidden, from_col, w_col)
    return (hidden, jnp.stack([flow_row, flow_col]))


BF = jnp.bfloat16
F32 = jnp.float32
MESH = pl.DeviceIdType.MESH
HALO = 4


def mm(a, b):
    return jnp.dot(a, b, preferred_element_type=F32)


def shifted_taps(padded, count):
    return jnp.concatenate(
        [padded[6 + k : 6 + k + count, :].astype(BF) for k in range(5)], axis=1
    )


def row_taps(value, step):
    zeros = jnp.zeros((2 * step, value.shape[1]), value.dtype)
    tall = jnp.concatenate([zeros, value, zeros], axis=0)
    count = value.shape[0]
    return jnp.concatenate([tall[k * step : k * step + count] for k in range(5)], axis=1)


def gate(x):
    return 0.5 * jnp.tanh(0.5 * x) + 0.5


def tap_weights(w_ref, first, low, high):
    return w_ref[:, first : first + 128, low:high].reshape(5 * 128, high - low)


def fused_kernel(
    bands,
    frame1_hbm,
    frame2_hbm,
    context_hbm,
    hidden_init_hbm,
    offsets_hbm,
    w_motion_hbm,
    w_row_hbm,
    w_col_hbm,
    hidden_out,
    flow_out,
    frame1,
    frame2,
    context,
    hidden_init,
    offsets,
    w_motion,
    w_row,
    w_col,
    strips,
    scores,
    ctx_stage,
    ctx_recv,
    flow_stage,
    flow_recv,
    hid_stage,
    hid_recv,
    out_stage,
    out_recv,
    pad_ctx,
    pad_hid,
    pad_mot,
    pad_gate,
    win_ctx,
    win_mot,
    win_hid,
    win_gate,
    acc_row,
    gate_row,
    acc_col,
    acc_row2,
    load_sem,
    strip_send,
    strip_recv,
    ctx_ssem,
    ctx_rsem,
    flow_ssem,
    flow_rsem,
    hid_ssem,
    hid_rsem,
    out_ssem,
    out_rsem,
):
    width = frame1.shape[0]
    own = width // bands
    win = own + 2 * HALO
    grid_cols = width // 8
    me = lax.axis_index("band")
    pair = lax.axis_index("pair")

    loads = [
        pltpu.make_async_copy(source, target, load_sem.at[i])
        for i, (source, target) in enumerate(
            (
                (frame2_hbm, frame2),
                (context_hbm, context),
                (hidden_init_hbm, hidden_init),
                (w_row_hbm, w_row),
                (frame1_hbm, frame1),
                (offsets_hbm, offsets),
                (w_motion_hbm, w_motion),
                (w_col_hbm, w_col),
            )
        )
    ]
    for load in loads:
        load.start()

    barrier = pltpu.get_barrier_semaphore()

    def greet(k, carry):
        pl.semaphore_signal(
            barrier, inc=1, device_id=(lax.rem(me + k, bands), pair), device_id_type=MESH
        )
        return carry

    lax.fori_loop(1, bands, greet, 0)

    loads[0].wait()
    blocks = frame2[...].astype(F32).reshape(grid_cols, 8, frame2.shape[1])
    strips[pl.ds(me, 1)] = (jnp.sum(blocks, axis=1) / 2.0).astype(BF)[None]

    def zero_ends(ref, count):
        ref[0:8, :] = jnp.zeros((8, 128), F32)
        ref[8 + count : 16 + count, :] = jnp.zeros((8, 128), F32)

    for ref in (pad_ctx, pad_hid, pad_mot, pad_gate):
        zero_ends(ref, width)
    for ref in (win_ctx, win_mot, win_hid, win_gate):
        zero_ends(ref, bands * win)

    loads[1].wait()
    loads[2].wait()
    pad_ctx[8 : 8 + width, :] = context[...].astype(F32)
    pad_hid[8 : 8 + width, :] = hidden_init[...].astype(F32)

    def stage_windows(stage, padded):
        for d in range(bands):
            first = 8 + own * d - HALO
            stage[d] = padded[first : first + win, :].astype(BF)

    stage_windows(ctx_stage, pad_ctx)

    order = sorted(range(1, bands), key=lambda k: abs(2 * k - bands))

    def scatter(stage, recv, ssem, rsem):
        for k in order:
            to = lax.rem(me + k, bands)
            pltpu.make_async_remote_copy(
                src_ref=stage.at[to],
                dst_ref=recv.at[me],
                send_sem=ssem,
                recv_sem=rsem,
                device_id=(to, pair),
                device_id_type=MESH,
            ).start()

    def wait_bytes(ref, sem):
        most = ref.at[pl.ds(0, bands - 1)]
        pltpu.make_async_copy(most, most, sem).wait()

    def collect(stage, recv, rsem):
        wait_bytes(recv, rsem)
        half = stage.shape[1] // 2 if stage.shape[1] == win else 0

        def keep(i, carry):
            recv[pl.ds(me, 1), pl.ds(i * half, half)] = stage[pl.ds(me, 1), pl.ds(i * half, half)]
            return carry

        if half:
            lax.fori_loop(0, 2, keep, 0)
        else:
            recv[pl.ds(me, 1)] = stage[pl.ds(me, 1)]

    def sent(stage, ssem):
        wait_bytes(stage, ssem)

    pl.semaphore_wait(barrier, bands - 1)

    level = me // 4
    place = lax.rem(me, 4)
    core = lax.rem(me, 2)
    sibling = me + 1 - 2 * core
    across = me + 2 - 4 * lax.rem(me // 2, 2)
    levels = (
        level,
        level + 1 - 2 * lax.rem(level, 2),
        2 - level // 2,
        3 - 3 * (level // 2),
    )
    line = [4 * other + place for other in levels]
    across_line = [4 * other + (across - 4 * level) for other in levels]
    started = []

    def pass_on(block, to, slot):
        copy = pltpu.make_async_remote_copy(
            src_ref=strips.at[block],
            dst_ref=strips.at[block],
            send_sem=strip_send.at[slot],
            recv_sem=strip_recv.at[block],
            device_id=(to, pair),
            device_id_type=MESH,
        )
        copy.start()
        started.append(copy)

    def arrived(block):
        pltpu.make_async_remote_copy(
            src_ref=strips.at[block],
            dst_ref=strips.at[block],
            send_sem=strip_send.at[0],
            recv_sem=strip_recv.at[block],
            device_id=(sibling, pair),
            device_id_type=MESH,
        ).wait_recv()

    pass_on(me, line[1], 0)
    pass_on(me, across, 1)
    pass_on(me, line[2], 2)
    pass_on(me, line[3], 3)
    pass_on(me, sibling, 4)

    loads[3].wait()
    gate_row[...] = mm(shifted_taps(pad_hid, width), tap_weights(w_row, 0, 0, 256))

    for i in (1, 2, 3):
        arrived(line[i])
        pass_on(line[i], across, 4 + i)
        pass_on(line[i], sibling, 7 + i)
    acc_row[...] = mm(shifted_taps(pad_ctx, width), tap_weights(w_row, 128, 0, 384))
    for i in (0, 1, 2, 3):
        arrived(across_line[i])
        pass_on(across_line[i], sibling, 11 + i)
    for i in (0, 1, 2, 3):
        arrived(line[i] + 1 - 2 * core)
    for i in (0, 1, 2, 3):
        arrived(across_line[i] + 1 - 2 * core)

    scatter(ctx_stage, ctx_recv, ctx_ssem, ctx_rsem)
    for load in loads[4:7]:
        load.wait()
    scores[...] = lax.dot_general(
        strips[...].reshape(bands * grid_cols, frame1.shape[1]),
        frame1[...],
        (((1,), (1,)), ((), ())),
        preferred_element_type=F32,
    ) * (1.0 / math.sqrt(frame1.shape[1]))

    row_f = me.astype(F32) / bands
    parts = []
    strip_ids = lax.broadcasted_iota(jnp.int32, (grid_cols, 128), 0)
    centres = ((8 * strip_ids).astype(F32) + 3.5) / width
    for lanes in range(0, width, 128):
        cut = slice(lanes, lanes + 128)
        column = lanes + lax.broadcasted_iota(jnp.int32, (1, 128), 1)
        target_row = me + offsets[0, :, cut]
        target_col = column // 8 + offsets[1, :, cut]
        inside = (
            (target_row >= 0)
            & (target_row < bands)
            & (target_col >= 0)
            & (target_col < grid_cols)
        )
        target = jnp.where(inside, target_row * grid_cols + target_col, -1)
        highest = scores[0:grid_cols, cut]
        for r in range(1, bands):
            highest = jnp.maximum(highest, scores[r * grid_cols : (r + 1) * grid_cols, cut])
        highest = jnp.max(highest, axis=0, keepdims=True)
        by_col = jnp.zeros((grid_cols, 128), F32)
        by_row = jnp.zeros((8, 128), F32)
        found = jnp.zeros((grid_cols, 128), F32)
        for r in range(bands):
            block = scores[r * grid_cols : (r + 1) * grid_cols, cut]
            raised = jnp.exp(block - highest)
            by_col = by_col + raised
            if r:
                folded = jnp.sum(raised.reshape(grid_cols // 8, 8, 128), axis=0)
                by_row = by_row + folded * (r / bands)
            found = found + jnp.where(strip_ids + r * grid_cols == target, block, 0.0)
        total = jnp.sum(by_col, axis=0, keepdims=True)
        moved_row = jnp.sum(by_row, axis=0, keepdims=True) / total
        moved_col = jnp.sum(by_col * centres, axis=0, keepdims=True) / total
        flow_row = moved_row - row_f
        flow_col = moved_col - column.astype(F32) / width
        flow_out[0, :, cut] = flow_row
        flow_out[1, :, cut] = flow_col
        parts.append(
            jnp.concatenate(
                [
                    flow_row,
                    flow_col,
                    jnp.sum(found, axis=0, keepdims=True),
                    jnp.zeros((5, 128), F32),
                ],
                axis=0,
            )
        )

    three = jnp.concatenate(parts + [jnp.zeros((8, 128), F32)], axis=1)
    span = width + 128
    line_id = lax.broadcasted_iota(jnp.int32, (8, span), 0)
    spread = jnp.where(line_id == 1, pltpu.roll(three, 32, 1), three)
    spread = jnp.where(line_id == 2, pltpu.roll(three, 64, 1), spread)
    lane_group = lax.broadcasted_iota(jnp.int32, (8, 128), 1) // 32
    wanted = lane_group == lax.broadcasted_iota(jnp.int32, (8, 128), 0)
    for d in range(bands):
        turned = pltpu.roll(spread, (span - (own * d - HALO)) % span, 1)[:, 0:128]
        flow_stage[d] = jnp.sum(jnp.where(wanted, turned, 0.0), axis=0, keepdims=True)
    scatter(flow_stage, flow_recv, flow_ssem, flow_rsem)

    def motion_of(first, second, third):
        return jnp.maximum(
            first * w_motion[0:1, :] + second * w_motion[1:2, :] + third * w_motion[2:3, :],
            0.0,
        )

    for i, part in enumerate(parts):
        upright = jnp.concatenate([part, jnp.zeros((120, 128), F32)], axis=0).T
        pad_mot[8 + 128 * i : 136 + 128 * i, :] = motion_of(
            upright[:, 0:1], upright[:, 1:2], upright[:, 2:3]
        )
    acc = mm(shifted_taps(pad_mot, width), tap_weights(w_row, 256, 0, 384)) + acc_row[...]
    start = pad_hid[8 : 8 + width, :]
    update = gate(gate_row[:, 0:128] + acc[:, 0:128])
    reset = gate(gate_row[:, 128:256] + acc[:, 128:256])
    pad_gate[8 : 8 + width, :] = reset * start
    candidate = jnp.tanh(
        mm(shifted_taps(pad_gate, width), tap_weights(w_row, 0, 256, 384)) + acc[:, 256:384]
    )
    pad_hid[8 : 8 + width, :] = (1.0 - update) * start + update * candidate
    stage_windows(hid_stage, pad_hid)
    scatter(hid_stage, hid_recv, hid_ssem, hid_rsem)

    pixels = bands * win
    collect(ctx_stage, ctx_recv, ctx_rsem)
    loads[7].wait()
    ctx = ctx_recv[...].reshape(pixels, 128)
    win_ctx[8 : 8 + pixels, :] = ctx.astype(F32)
    acc_col[...] = mm(row_taps(ctx, win), tap_weights(w_col, 128, 0, 384))
    acc_row2[...] = mm(shifted_taps(win_ctx, pixels), tap_weights(w_row, 128, 0, 384))
    collect(flow_stage, flow_recv, flow_rsem)
    upright = jnp.concatenate(
        [flow_recv[r] for r in range(bands)] + [jnp.zeros((128 - bands, 128), F32)], axis=0
    ).T
    for r in range(bands):
        win_mot[8 + win * r : 8 + win * (r + 1), :] = motion_of(
            upright[0:win, r : r + 1],
            upright[win : 2 * win, r : r + 1],
            upright[2 * win : 3 * win, r : r + 1],
        )
    motion = win_mot[8 : 8 + pixels, :].astype(BF)
    acc_col[...] += mm(row_taps(motion, win), tap_weights(w_col, 256, 0, 384))
    acc_row2[...] += mm(shifted_taps(win_mot, pixels), tap_weights(w_row, 256, 0, 384))

    collect(hid_stage, hid_recv, hid_rsem)
    state_half = hid_recv[...].reshape(pixels, 128)
    state = state_half.astype(F32)

    def gru(state, half, acc, weight, taps_of):
        pre = mm(taps_of(half, win_hid), tap_weights(weight, 0, 0, 256)) + acc[:, 0:256]
        update = gate(pre[:, 0:128])
        reset = gate(pre[:, 128:256])
        gated = (reset * half.astype(F32)).astype(BF)
        candidate = jnp.tanh(
            mm(taps_of(gated, win_gate), tap_weights(weight, 0, 256, 384)) + acc[:, 256:384]
        )
        return (1.0 - update) * state + update * candidate

    def taps_down(value, unused):
        return row_taps(value, win)

    def taps_along(value, padded):
        padded[8 : 8 + pixels, :] = value.astype(F32)
        return shifted_taps(padded, pixels)

    state = gru(state, state_half, acc_col, w_col, taps_down)
    state = gru(state, state.astype(BF), acc_row2, w_row, taps_along)
    state = gru(state, state.astype(BF), acc_col, w_col, taps_down)
    win_hid[8 : 8 + pixels, :] = state
    for r in range(bands):
        first = 8 + win * r + HALO
        out_stage[r] = win_hid[first : first + own, :].astype(BF)
    scatter(out_stage, out_recv, out_ssem, out_rsem)
    for copy in started:
        copy.wait_send()
    sent(ctx_stage, ctx_ssem)
    sent(flow_stage, flow_ssem)
    sent(hid_stage, hid_ssem)
    collect(out_stage, out_recv, out_rsem)
    hidden_out[...] = out_recv[...]
    sent(out_stage, out_ssem)


def per_device_columns(
    bands, frame1, frame2, context, hidden_init, offsets, w_motion, w_row, w_col
):
    unused, width, channels = frame1.shape
    own = width // bands
    win = own + 2 * HALO
    pixels = bands * win
    vmem = pl.BlockSpec(memory_space=pltpu.VMEM)
    hbm = pl.BlockSpec(memory_space=pltpu.HBM)
    dma = pltpu.SemaphoreType.DMA
    tall = pltpu.VMEM((width + 16, 128), F32)
    wide = pltpu.VMEM((pixels + 16, 128), F32)
    hidden, flow = pl.pallas_call(
        functools.partial(fused_kernel, bands),
        out_shape=(
            jax.ShapeDtypeStruct((bands, own, 128), BF),
            jax.ShapeDtypeStruct((2, 1, width), F32),
        ),
        in_specs=[hbm] * 8,
        out_specs=(vmem, vmem),
        scratch_shapes=[
            pltpu.VMEM((width, channels), BF),
            pltpu.VMEM((width, channels), BF),
            pltpu.VMEM((width, 128), BF),
            pltpu.VMEM((width, 128), BF),
            pltpu.VMEM(offsets.shape, jnp.int32),
            pltpu.VMEM(w_motion.shape, F32),
            pltpu.VMEM(w_row.shape, BF),
            pltpu.VMEM(w_col.shape, BF),
            pltpu.VMEM((bands, width // 8, channels), BF),
            pltpu.VMEM((bands * width // 8, width), F32),
            pltpu.VMEM((bands, win, 128), BF),
            pltpu.VMEM((bands, win, 128), BF),
            pltpu.VMEM((bands, 1, 128), F32),
            pltpu.VMEM((bands, 1, 128), F32),
            pltpu.VMEM((bands, win, 128), BF),
            pltpu.VMEM((bands, win, 128), BF),
            pltpu.VMEM((bands, own, 128), BF),
            pltpu.VMEM((bands, own, 128), BF),
            tall,
            tall,
            tall,
            tall,
            wide,
            wide,
            wide,
            wide,
            pltpu.VMEM((width, 384), F32),
            pltpu.VMEM((width, 256), F32),
            pltpu.VMEM((pixels, 384), F32),
            pltpu.VMEM((pixels, 384), F32),
            dma((8,)),
            dma((15,)),
            dma((bands,)),
        ]
        + [dma] * 8,
        compiler_params=pltpu.CompilerParams(
            collective_id=0, has_side_effects=True, vmem_limit_bytes=63 * 1024 * 1024
        ),
        cost_estimate=pl.CostEstimate(
            flops=2_400_000_000, bytes_accessed=4_500_000, transcendentals=700_000
        ),
    )(
        frame1.reshape(width, channels),
        frame2.reshape(width, channels),
        context.reshape(width, 128),
        hidden_init.reshape(width, 128),
        offsets,
        w_motion,
        w_row,
        w_col,
    )
    return (hidden.astype(F32).reshape(1, width, 128), flow)


def solution(mesh):
    bands = mesh.shape["band"]

    def per_device(frame1, frame2, *rest):
        own = frame1.shape[1] // bands
        if bands == 16 and frame1.shape[0] == 1 and own + 2 * HALO == 32:
            return per_device_columns(bands, frame1, frame2, *rest)
        return per_device_rows(frame1, frame2, *rest)

    return jax.shard_map(
        per_device,
        mesh=mesh,
        in_specs=(
            P("band", "pair", None),
            P("band", "pair", None),
            P("band", "pair", None),
            P("band", "pair", None),
            P(None, "band", "pair"),
            P(),
            P(),
            P(),
        ),
        out_specs=(P("band", "pair", None), P(None, "band", "pair")),
        check_vma=False,
    )
```

```python
import functools
import math

import jax
import jax.numpy as jnp
from jax import lax
from jax.experimental import pallas as pl
from jax.experimental.pallas import tpu as pltpu
from jax.sharding import PartitionSpec as P

ITERS = 2


def passed_along(array, axis, by):
    count = lax.axis_size(axis)
    pairs = [(i, i + by) for i in range(count) if 0 <= i + by < count]
    return lax.ppermute(array, axis, pairs)


def pool_strips(frame2):
    band_rows, image_width, channels = frame2.shape
    blocks = frame2.astype(jnp.float32).reshape(band_rows, image_width // 8, 8, channels)
    return (jnp.sum(blocks, axis=2) / 2.0).astype(jnp.bfloat16)


def lookup_targets(offsets, row_first, total_rows, image_width):
    band_rows = offsets.shape[1]
    pixel_row = (
        row_first
        + jnp.arange(band_rows, dtype=jnp.int32)[:, None]
        + jnp.zeros((1, image_width), jnp.int32)
    )
    pixel_col = jnp.arange(image_width, dtype=jnp.int32)[None, :]
    target_row = pixel_row + offsets[0]
    target_col = pixel_col // 8 + offsets[1]
    inside = (
        (target_row >= 0)
        & (target_row < total_rows)
        & (target_col >= 0)
        & (target_col < image_width // 8)
    )
    target_row = jnp.where(inside, target_row, -1)
    target_col = jnp.where(inside, target_col, -1)
    return (target_row, target_col, pixel_row, pixel_col)


def strip_step(
    state, feature_rows, strip_block, row_zero, total_rows, image_width, target_row, target_col
):
    block_rows, grid_cols, channels = strip_block.shape
    scores = jnp.dot(
        feature_rows,
        strip_block.reshape(block_rows * grid_cols, channels).T,
        preferred_element_type=jnp.float32,
    ) / math.sqrt(channels)
    running_max, denominator, acc_row, acc_col, lookup = state
    new_max = jnp.maximum(running_max, jnp.max(scores, axis=1))
    shrink = jnp.exp(running_max - new_max)
    exponent = jnp.exp(scores - new_max[:, None]).reshape(-1, block_rows, grid_cols)
    strip_row = row_zero + jnp.arange(block_rows, dtype=jnp.int32)
    column_ids = jnp.arange(grid_cols, dtype=jnp.int32)
    row_centre = strip_row.astype(jnp.float32) / total_rows
    col_centre = ((8 * column_ids).astype(jnp.float32) + 3.5) / image_width
    row_weight = jnp.sum(exponent, axis=2)
    col_weight = jnp.sum(exponent, axis=1)
    scores_grid = scores.reshape(-1, block_rows, grid_cols)
    hit = (strip_row[None, :, None] == target_row[:, None, None]) & (
        column_ids[None, None, :] == target_col[:, None, None]
    )
    found = jnp.sum(jnp.where(hit, scores_grid, 0.0), axis=(1, 2))
    return (
        new_max,
        denominator * shrink + jnp.sum(row_weight, axis=1),
        acc_row * shrink + jnp.sum(row_weight * row_centre[None, :], axis=1),
        acc_col * shrink + jnp.sum(col_weight * col_centre[None, :], axis=1),
        lookup + found,
    )


def conv_valid(source, weight, conv_axis):
    out_count = source.shape[conv_axis] - 4
    summed = None
    for kernel_tap in range(5):
        tap_slice = lax.slice_in_dim(source, kernel_tap, kernel_tap + out_count, axis=conv_axis)
        tap_term = jnp.dot(
            tap_slice.reshape(-1, tap_slice.shape[-1]),
            weight[kernel_tap],
            preferred_element_type=jnp.float32,
        )
        summed = tap_term if summed is None else summed + tap_term
    out_shape = tuple(tap_slice.shape[:-1]) + (weight.shape[-1],)
    return summed.reshape(out_shape)


def pad_columns(source):
    return jnp.pad(source, ((0, 0), (2, 2), (0, 0)))


def rows_around(source, depth, mover):
    above = [
        mover(source, offset)
        for offset in list(range(depth, 0, -1)) + list(range(-1, -depth - 1, -1))
    ]
    return jnp.concatenate(above[:depth] + [source] + above[depth:], axis=0)


def row_pass(hidden, from_inputs, weight):
    width_h = hidden.shape[-1]
    hidden_half = lax.optimization_barrier(hidden.astype(jnp.bfloat16))
    gate_pair = jax.nn.sigmoid(
        conv_valid(pad_columns(hidden_half), weight[:, :width_h, : 2 * width_h], 1)
        + from_inputs[..., : 2 * width_h]
    )
    update_gate = gate_pair[..., :width_h]
    reset_gate = gate_pair[..., width_h:]
    gated = (reset_gate * hidden_half.astype(jnp.float32)).astype(jnp.bfloat16)
    candidate = jnp.tanh(
        conv_valid(pad_columns(gated), weight[:, :width_h, 2 * width_h :], 1)
        + from_inputs[..., 2 * width_h :]
    )
    return (1.0 - update_gate) * hidden + update_gate * candidate


def column_pass_each(hidden, from_inputs, weight):
    width_h = hidden.shape[-1]
    hidden_half = lax.optimization_barrier(hidden.astype(jnp.bfloat16))
    hidden_ext = rows_around(
        hidden_half, 2, lambda source, offset: passed_along(source, "band", offset)
    )
    gate_pair = jax.nn.sigmoid(
        conv_valid(hidden_ext, weight[:, :width_h, : 2 * width_h], 0)
        + from_inputs[..., : 2 * width_h]
    )
    update_gate = gate_pair[..., :width_h]
    reset_gate = gate_pair[..., width_h:]
    gated = (reset_gate * hidden_half.astype(jnp.float32)).astype(jnp.bfloat16)
    gated_ext = rows_around(gated, 2, lambda source, offset: passed_along(source, "band", offset))
    candidate = jnp.tanh(
        conv_valid(gated_ext, weight[:, :width_h, 2 * width_h :], 0)
        + from_inputs[..., 2 * width_h :]
    )
    return (1.0 - update_gate) * hidden + update_gate * candidate


def per_device_rows(frame1, frame2, context, hidden_init, offsets, w_motion, w_row, w_col):
    band_rows, image_width, channels = frame1.shape
    total_rows = band_rows * lax.axis_size("band")
    row_first = lax.axis_index("band") * band_rows
    strips = pool_strips(frame2)
    target_row, target_col, pixel_row, pixel_col = lookup_targets(
        offsets, row_first, total_rows, image_width
    )
    pixel_count = band_rows * image_width
    features = frame1.reshape(pixel_count, channels)
    rows_target = target_row.reshape(pixel_count)
    cols_target = target_col.reshape(pixel_count)
    zeros_state = jnp.zeros((pixel_count,), jnp.float32)
    initial = (
        jnp.full((pixel_count,), -jnp.inf, jnp.float32),
        zeros_state,
        zeros_state,
        zeros_state,
        zeros_state,
    )
    state = initial
    arriving = lax.all_gather(strips, "band", axis=0, tiled=True)
    arriving_rows = arriving.shape[0]
    step_rows = min(arriving_rows, 16)
    full_steps = arriving_rows // step_rows
    blocks = arriving.reshape((full_steps, step_rows) + arriving.shape[1:])
    starts = step_rows * jnp.arange(full_steps, dtype=jnp.int32)

    def advance(carry, pieces):
        return (
            strip_step(
                carry,
                features,
                pieces[0],
                pieces[1],
                total_rows,
                image_width,
                rows_target,
                cols_target,
            ),
            None,
        )

    state, unused = lax.scan(advance, state, (blocks, starts))
    running_max, denominator, acc_row, acc_col, lookup = state
    flow_row = (acc_row / denominator).reshape(band_rows, image_width) - pixel_row.astype(
        jnp.float32
    ) / total_rows
    flow_col = (acc_col / denominator).reshape(band_rows, image_width) - pixel_col.astype(
        jnp.float32
    ) / image_width
    lookup = lookup.reshape(band_rows, image_width)
    motion = jax.nn.relu(
        flow_row[..., None] * w_motion[0]
        + flow_col[..., None] * w_motion[1]
        + lookup[..., None] * w_motion[2]
    ).astype(jnp.bfloat16)
    inputs = jnp.concatenate([context, motion], axis=-1)
    width_h = hidden_init.shape[-1]
    from_row = conv_valid(pad_columns(inputs), w_row[:, width_h:, :], 1)
    hidden = hidden_init.astype(jnp.float32)
    inputs_ext = rows_around(inputs, 2, lambda source, offset: passed_along(source, "band", offset))
    from_col = conv_valid(inputs_ext, w_col[:, width_h:, :], 0)
    for iteration in range(ITERS):
        hidden = row_pass(hidden, from_row, w_row)
        hidden = column_pass_each(hidden, from_col, w_col)
    return (hidden, jnp.stack([flow_row, flow_col]))


BF = jnp.bfloat16
F32 = jnp.float32
MESH = pl.DeviceIdType.MESH
HALO = 4


def mm(a, b):
    return jnp.dot(a, b, preferred_element_type=F32)


def shifted_taps(padded, count):
    return jnp.concatenate(
        [padded[6 + k : 6 + k + count, :].astype(BF) for k in range(5)], axis=1
    )


def row_taps(value, step):
    zeros = jnp.zeros((2 * step, value.shape[1]), value.dtype)
    tall = jnp.concatenate([zeros, value, zeros], axis=0)
    count = value.shape[0]
    return jnp.concatenate([tall[k * step : k * step + count] for k in range(5)], axis=1)


def gate(x):
    return 0.5 * jnp.tanh(0.5 * x) + 0.5


def tap_weights(w_ref, first, low, high):
    return w_ref[:, first : first + 128, low:high].reshape(5 * 128, high - low)


def fused_kernel(
    bands,
    frame1_hbm,
    frame2_hbm,
    context_hbm,
    hidden_init_hbm,
    offsets_hbm,
    w_motion_hbm,
    w_row_hbm,
    w_col_hbm,
    hidden_out,
    flow_out,
    frame1,
    frame2,
    context,
    hidden_init,
    offsets,
    w_motion,
    w_row,
    w_col,
    strips,
    scores,
    ctx_stage,
    ctx_recv,
    flow_stage,
    flow_recv,
    hid_stage,
    hid_recv,
    out_stage,
    out_recv,
    pad_ctx,
    pad_hid,
    pad_mot,
    pad_gate,
    win_ctx,
    win_mot,
    win_hid,
    win_gate,
    acc_row,
    gate_row,
    acc_col,
    acc_row2,
    load_sem,
    strip_send,
    strip_recv,
    ctx_ssem,
    ctx_rsem,
    flow_ssem,
    flow_rsem,
    hid_ssem,
    hid_rsem,
    out_ssem,
    out_rsem,
):
    width = frame1.shape[0]
    own = width // bands
    win = own + 2 * HALO
    grid_cols = width // 8
    me = lax.axis_index("band")
    pair = lax.axis_index("pair")

    loads = [
        pltpu.make_async_copy(source, target, load_sem.at[i])
        for i, (source, target) in enumerate(
            (
                (frame2_hbm, frame2),
                (context_hbm, context),
                (hidden_init_hbm, hidden_init),
                (w_row_hbm, w_row),
                (frame1_hbm, frame1),
                (offsets_hbm, offsets),
                (w_motion_hbm, w_motion),
                (w_col_hbm, w_col),
            )
        )
    ]
    for load in loads:
        load.start()

    barrier = pltpu.get_barrier_semaphore()

    def greet(k, carry):
        pl.semaphore_signal(
            barrier, inc=1, device_id=(lax.rem(me + k, bands), pair), device_id_type=MESH
        )
        return carry

    lax.fori_loop(1, bands, greet, 0)

    loads[0].wait()
    blocks = frame2[...].astype(F32).reshape(grid_cols, 8, frame2.shape[1])
    strips[pl.ds(me, 1)] = (jnp.sum(blocks, axis=1) / 2.0).astype(BF)[None]

    def zero_ends(ref, count):
        ref[0:8, :] = jnp.zeros((8, 128), F32)
        ref[8 + count : 16 + count, :] = jnp.zeros((8, 128), F32)

    for ref in (pad_ctx, pad_hid, pad_mot, pad_gate):
        zero_ends(ref, width)
    for ref in (win_ctx, win_mot, win_hid, win_gate):
        zero_ends(ref, bands * win)

    loads[1].wait()
    loads[2].wait()
    pad_ctx[8 : 8 + width, :] = context[...].astype(F32)
    pad_hid[8 : 8 + width, :] = hidden_init[...].astype(F32)

    def stage_windows(stage, padded):
        for d in range(bands):
            first = 8 + own * d - HALO
            stage[d] = padded[first : first + win, :].astype(BF)

    stage_windows(ctx_stage, pad_ctx)

    order = sorted(range(1, bands), key=lambda k: abs(2 * k - bands))

    def scatter(stage, recv, ssem, rsem):
        for k in order:
            to = lax.rem(me + k, bands)
            pltpu.make_async_remote_copy(
                src_ref=stage.at[to],
                dst_ref=recv.at[me],
                send_sem=ssem,
                recv_sem=rsem,
                device_id=(to, pair),
                device_id_type=MESH,
            ).start()

    def wait_bytes(ref, sem):
        most = ref.at[pl.ds(0, bands - 1)]
        pltpu.make_async_copy(most, most, sem).wait()

    def collect(stage, recv, rsem):
        wait_bytes(recv, rsem)
        half = stage.shape[1] // 2 if stage.shape[1] == win else 0

        def keep(i, carry):
            recv[pl.ds(me, 1), pl.ds(i * half, half)] = stage[pl.ds(me, 1), pl.ds(i * half, half)]
            return carry

        if half:
            lax.fori_loop(0, 2, keep, 0)
        else:
            recv[pl.ds(me, 1)] = stage[pl.ds(me, 1)]

    def sent(stage, ssem):
        wait_bytes(stage, ssem)

    pl.semaphore_wait(barrier, bands - 1)

    level = me // 4
    place = lax.rem(me, 4)
    core = lax.rem(me, 2)
    sibling = me + 1 - 2 * core
    across = me + 2 - 4 * lax.rem(me // 2, 2)
    levels = (
        level,
        level + 1 - 2 * lax.rem(level, 2),
        2 - level // 2,
        3 - 3 * (level // 2),
    )
    line = [4 * other + place for other in levels]
    across_line = [4 * other + (across - 4 * level) for other in levels]
    started = []

    def pass_on(block, to, slot):
        copy = pltpu.make_async_remote_copy(
            src_ref=strips.at[block],
            dst_ref=strips.at[block],
            send_sem=strip_send.at[slot],
            recv_sem=strip_recv.at[block],
            device_id=(to, pair),
            device_id_type=MESH,
        )
        copy.start()
        started.append(copy)

    def arrived(block):
        pltpu.make_async_remote_copy(
            src_ref=strips.at[block],
            dst_ref=strips.at[block],
            send_sem=strip_send.at[0],
            recv_sem=strip_recv.at[block],
            device_id=(sibling, pair),
            device_id_type=MESH,
        ).wait_recv()

    pass_on(me, across, 1)
    pass_on(me, line[1], 0)
    pass_on(me, line[2], 2)
    pass_on(me, line[3], 3)
    pass_on(me, sibling, 4)

    loads[3].wait()
    gate_row[...] = mm(shifted_taps(pad_hid, width), tap_weights(w_row, 0, 0, 256))

    for i in (1, 2, 3):
        arrived(line[i])
        pass_on(line[i], across, 4 + i)
        pass_on(line[i], sibling, 7 + i)
    acc_row[...] = mm(shifted_taps(pad_ctx, width), tap_weights(w_row, 128, 0, 384))
    for i in (0, 1, 2, 3):
        arrived(across_line[i])
        pass_on(across_line[i], sibling, 11 + i)
    scatter(ctx_stage, ctx_recv, ctx_ssem, ctx_rsem)
    for load in loads[4:7]:
        load.wait()
    for i in (0, 1, 2, 3):
        arrived(line[i] + 1 - 2 * core)
    for i in (0, 1, 2, 3):
        arrived(across_line[i] + 1 - 2 * core)

    scores[...] = lax.dot_general(
        strips[...].reshape(bands * grid_cols, frame1.shape[1]),
        frame1[...],
        (((1,), (1,)), ((), ())),
        preferred_element_type=F32,
    ) * (1.0 / math.sqrt(frame1.shape[1]))

    row_f = me.astype(F32) / bands
    parts = []
    strip_ids = lax.broadcasted_iota(jnp.int32, (grid_cols, 128), 0)
    centres = ((8 * strip_ids).astype(F32) + 3.5) / width
    for lanes in range(0, width, 128):
        cut = slice(lanes, lanes + 128)
        column = lanes + lax.broadcasted_iota(jnp.int32, (1, 128), 1)
        target_row = me + offsets[0, :, cut]
        target_col = column // 8 + offsets[1, :, cut]
        inside = (
            (target_row >= 0)
            & (target_row < bands)
            & (target_col >= 0)
            & (target_col < grid_cols)
        )
        target = jnp.where(inside, target_row * grid_cols + target_col, -1)
        highest = scores[0:grid_cols, cut]
        for r in range(1, bands):
            highest = jnp.maximum(highest, scores[r * grid_cols : (r + 1) * grid_cols, cut])
        highest = jnp.max(highest, axis=0, keepdims=True)
        by_col = jnp.zeros((grid_cols, 128), F32)
        by_row = jnp.zeros((8, 128), F32)
        found = jnp.zeros((grid_cols, 128), F32)
        for r in range(bands):
            block = scores[r * grid_cols : (r + 1) * grid_cols, cut]
            raised = jnp.exp(block - highest)
            by_col = by_col + raised
            if r:
                folded = jnp.sum(raised.reshape(grid_cols // 8, 8, 128), axis=0)
                by_row = by_row + folded * (r / bands)
            found = found + jnp.where(strip_ids + r * grid_cols == target, block, 0.0)
        total = jnp.sum(by_col, axis=0, keepdims=True)
        moved_row = jnp.sum(by_row, axis=0, keepdims=True) / total
        moved_col = jnp.sum(by_col * centres, axis=0, keepdims=True) / total
        flow_row = moved_row - row_f
        flow_col = moved_col - column.astype(F32) / width
        flow_out[0, :, cut] = flow_row
        flow_out[1, :, cut] = flow_col
        parts.append(
            jnp.concatenate(
                [
                    flow_row,
                    flow_col,
                    jnp.sum(found, axis=0, keepdims=True),
                    jnp.zeros((5, 128), F32),
                ],
                axis=0,
            )
        )

    three = jnp.concatenate(parts + [jnp.zeros((8, 128), F32)], axis=1)
    span = width + 128
    line_id = lax.broadcasted_iota(jnp.int32, (8, span), 0)
    spread = jnp.where(line_id == 1, pltpu.roll(three, 32, 1), three)
    spread = jnp.where(line_id == 2, pltpu.roll(three, 64, 1), spread)
    lane_group = lax.broadcasted_iota(jnp.int32, (8, 128), 1) // 32
    wanted = lane_group == lax.broadcasted_iota(jnp.int32, (8, 128), 0)
    for d in range(bands):
        turned = pltpu.roll(spread, (span - (own * d - HALO)) % span, 1)[:, 0:128]
        flow_stage[d] = jnp.sum(jnp.where(wanted, turned, 0.0), axis=0, keepdims=True)
    scatter(flow_stage, flow_recv, flow_ssem, flow_rsem)

    def motion_of(first, second, third):
        return jnp.maximum(
            first * w_motion[0:1, :] + second * w_motion[1:2, :] + third * w_motion[2:3, :],
            0.0,
        )

    for i, part in enumerate(parts):
        upright = jnp.concatenate([part, jnp.zeros((120, 128), F32)], axis=0).T
        pad_mot[8 + 128 * i : 136 + 128 * i, :] = motion_of(
            upright[:, 0:1], upright[:, 1:2], upright[:, 2:3]
        )
    acc = mm(shifted_taps(pad_mot, width), tap_weights(w_row, 256, 0, 384)) + acc_row[...]
    start = pad_hid[8 : 8 + width, :]
    update = gate(gate_row[:, 0:128] + acc[:, 0:128])
    reset = gate(gate_row[:, 128:256] + acc[:, 128:256])
    pad_gate[8 : 8 + width, :] = reset * start
    candidate = jnp.tanh(
        mm(shifted_taps(pad_gate, width), tap_weights(w_row, 0, 256, 384)) + acc[:, 256:384]
    )
    pad_hid[8 : 8 + width, :] = (1.0 - update) * start + update * candidate
    stage_windows(hid_stage, pad_hid)
    scatter(hid_stage, hid_recv, hid_ssem, hid_rsem)

    pixels = bands * win
    collect(ctx_stage, ctx_recv, ctx_rsem)
    loads[7].wait()
    ctx = ctx_recv[...].reshape(pixels, 128)
    win_ctx[8 : 8 + pixels, :] = ctx.astype(F32)
    acc_col[...] = mm(row_taps(ctx, win), tap_weights(w_col, 128, 0, 384))
    acc_row2[...] = mm(shifted_taps(win_ctx, pixels), tap_weights(w_row, 128, 0, 384))
    collect(flow_stage, flow_recv, flow_rsem)
    upright = jnp.concatenate(
        [flow_recv[r] for r in range(bands)] + [jnp.zeros((128 - bands, 128), F32)], axis=0
    ).T
    for r in range(bands):
        win_mot[8 + win * r : 8 + win * (r + 1), :] = motion_of(
            upright[0:win, r : r + 1],
            upright[win : 2 * win, r : r + 1],
            upright[2 * win : 3 * win, r : r + 1],
        )
    motion = win_mot[8 : 8 + pixels, :].astype(BF)
    acc_col[...] += mm(row_taps(motion, win), tap_weights(w_col, 256, 0, 384))
    acc_row2[...] += mm(shifted_taps(win_mot, pixels), tap_weights(w_row, 256, 0, 384))

    collect(hid_stage, hid_recv, hid_rsem)
    state_half = hid_recv[...].reshape(pixels, 128)
    state = state_half.astype(F32)

    def gru(state, half, acc, weight, taps_of):
        pre = mm(taps_of(half, win_hid), tap_weights(weight, 0, 0, 256)) + acc[:, 0:256]
        update = gate(pre[:, 0:128])
        reset = gate(pre[:, 128:256])
        gated = (reset * half.astype(F32)).astype(BF)
        candidate = jnp.tanh(
            mm(taps_of(gated, win_gate), tap_weights(weight, 0, 256, 384)) + acc[:, 256:384]
        )
        return (1.0 - update) * state + update * candidate

    def taps_down(value, unused):
        return row_taps(value, win)

    def taps_along(value, padded):
        padded[8 : 8 + pixels, :] = value.astype(F32)
        return shifted_taps(padded, pixels)

    state = gru(state, state_half, acc_col, w_col, taps_down)
    state = gru(state, state.astype(BF), acc_row2, w_row, taps_along)
    state = gru(state, state.astype(BF), acc_col, w_col, taps_down)
    win_hid[8 : 8 + pixels, :] = state
    for r in range(bands):
        first = 8 + win * r + HALO
        out_stage[r] = win_hid[first : first + own, :].astype(BF)
    scatter(out_stage, out_recv, out_ssem, out_rsem)
    for copy in started:
        copy.wait_send()
    sent(ctx_stage, ctx_ssem)
    sent(flow_stage, flow_ssem)
    sent(hid_stage, hid_ssem)
    collect(out_stage, out_recv, out_rsem)
    hidden_out[...] = out_recv[...]
    sent(out_stage, out_ssem)


def per_device_columns(
    bands, frame1, frame2, context, hidden_init, offsets, w_motion, w_row, w_col
):
    unused, width, channels = frame1.shape
    own = width // bands
    win = own + 2 * HALO
    pixels = bands * win
    vmem = pl.BlockSpec(memory_space=pltpu.VMEM)
    hbm = pl.BlockSpec(memory_space=pltpu.HBM)
    dma = pltpu.SemaphoreType.DMA
    tall = pltpu.VMEM((width + 16, 128), F32)
    wide = pltpu.VMEM((pixels + 16, 128), F32)
    hidden, flow = pl.pallas_call(
        functools.partial(fused_kernel, bands),
        out_shape=(
            jax.ShapeDtypeStruct((bands, own, 128), BF),
            jax.ShapeDtypeStruct((2, 1, width), F32),
        ),
        in_specs=[hbm] * 8,
        out_specs=(vmem, vmem),
        scratch_shapes=[
            pltpu.VMEM((width, channels), BF),
            pltpu.VMEM((width, channels), BF),
            pltpu.VMEM((width, 128), BF),
            pltpu.VMEM((width, 128), BF),
            pltpu.VMEM(offsets.shape, jnp.int32),
            pltpu.VMEM(w_motion.shape, F32),
            pltpu.VMEM(w_row.shape, BF),
            pltpu.VMEM(w_col.shape, BF),
            pltpu.VMEM((bands, width // 8, channels), BF),
            pltpu.VMEM((bands * width // 8, width), F32),
            pltpu.VMEM((bands, win, 128), BF),
            pltpu.VMEM((bands, win, 128), BF),
            pltpu.VMEM((bands, 1, 128), F32),
            pltpu.VMEM((bands, 1, 128), F32),
            pltpu.VMEM((bands, win, 128), BF),
            pltpu.VMEM((bands, win, 128), BF),
            pltpu.VMEM((bands, own, 128), BF),
            pltpu.VMEM((bands, own, 128), BF),
            tall,
            tall,
            tall,
            tall,
            wide,
            wide,
            wide,
            wide,
            pltpu.VMEM((width, 384), F32),
            pltpu.VMEM((width, 256), F32),
            pltpu.VMEM((pixels, 384), F32),
            pltpu.VMEM((pixels, 384), F32),
            dma((8,)),
            dma((15,)),
            dma((bands,)),
        ]
        + [dma] * 8,
        compiler_params=pltpu.CompilerParams(
            collective_id=0, has_side_effects=True, vmem_limit_bytes=63 * 1024 * 1024
        ),
        cost_estimate=pl.CostEstimate(
            flops=2_400_000_000, bytes_accessed=4_500_000, transcendentals=700_000
        ),
    )(
        frame1.reshape(width, channels),
        frame2.reshape(width, channels),
        context.reshape(width, 128),
        hidden_init.reshape(width, 128),
        offsets,
        w_motion,
        w_row,
        w_col,
    )
    return (hidden.astype(F32).reshape(1, width, 128), flow)


def solution(mesh):
    bands = mesh.shape["band"]

    def per_device(frame1, frame2, *rest):
        own = frame1.shape[1] // bands
        if bands == 16 and frame1.shape[0] == 1 and own + 2 * HALO == 32:
            return per_device_columns(bands, frame1, frame2, *rest)
        return per_device_rows(frame1, frame2, *rest)

    return jax.shard_map(
        per_device,
        mesh=mesh,
        in_specs=(
            P("band", "pair", None),
            P("band", "pair", None),
            P("band", "pair", None),
            P("band", "pair", None),
            P(None, "band", "pair"),
            P(),
            P(),
            P(),
        ),
        out_specs=(P("band", "pair", None), P(None, "band", "pair")),
        check_vma=False,
    )
```

```python
import functools
import math

import jax
import jax.numpy as jnp
from jax import lax
from jax.experimental import pallas as pl
from jax.experimental.pallas import tpu as pltpu
from jax.sharding import PartitionSpec as P

ITERS = 2


def passed_along(array, axis, by):
    count = lax.axis_size(axis)
    pairs = [(i, i + by) for i in range(count) if 0 <= i + by < count]
    return lax.ppermute(array, axis, pairs)


def pool_strips(frame2):
    band_rows, image_width, channels = frame2.shape
    blocks = frame2.astype(jnp.float32).reshape(band_rows, image_width // 8, 8, channels)
    return (jnp.sum(blocks, axis=2) / 2.0).astype(jnp.bfloat16)


def lookup_targets(offsets, row_first, total_rows, image_width):
    band_rows = offsets.shape[1]
    pixel_row = (
        row_first
        + jnp.arange(band_rows, dtype=jnp.int32)[:, None]
        + jnp.zeros((1, image_width), jnp.int32)
    )
    pixel_col = jnp.arange(image_width, dtype=jnp.int32)[None, :]
    target_row = pixel_row + offsets[0]
    target_col = pixel_col // 8 + offsets[1]
    inside = (
        (target_row >= 0)
        & (target_row < total_rows)
        & (target_col >= 0)
        & (target_col < image_width // 8)
    )
    target_row = jnp.where(inside, target_row, -1)
    target_col = jnp.where(inside, target_col, -1)
    return (target_row, target_col, pixel_row, pixel_col)


def strip_step(
    state, feature_rows, strip_block, row_zero, total_rows, image_width, target_row, target_col
):
    block_rows, grid_cols, channels = strip_block.shape
    scores = jnp.dot(
        feature_rows,
        strip_block.reshape(block_rows * grid_cols, channels).T,
        preferred_element_type=jnp.float32,
    ) / math.sqrt(channels)
    running_max, denominator, acc_row, acc_col, lookup = state
    new_max = jnp.maximum(running_max, jnp.max(scores, axis=1))
    shrink = jnp.exp(running_max - new_max)
    exponent = jnp.exp(scores - new_max[:, None]).reshape(-1, block_rows, grid_cols)
    strip_row = row_zero + jnp.arange(block_rows, dtype=jnp.int32)
    column_ids = jnp.arange(grid_cols, dtype=jnp.int32)
    row_centre = strip_row.astype(jnp.float32) / total_rows
    col_centre = ((8 * column_ids).astype(jnp.float32) + 3.5) / image_width
    row_weight = jnp.sum(exponent, axis=2)
    col_weight = jnp.sum(exponent, axis=1)
    scores_grid = scores.reshape(-1, block_rows, grid_cols)
    hit = (strip_row[None, :, None] == target_row[:, None, None]) & (
        column_ids[None, None, :] == target_col[:, None, None]
    )
    found = jnp.sum(jnp.where(hit, scores_grid, 0.0), axis=(1, 2))
    return (
        new_max,
        denominator * shrink + jnp.sum(row_weight, axis=1),
        acc_row * shrink + jnp.sum(row_weight * row_centre[None, :], axis=1),
        acc_col * shrink + jnp.sum(col_weight * col_centre[None, :], axis=1),
        lookup + found,
    )


def conv_valid(source, weight, conv_axis):
    out_count = source.shape[conv_axis] - 4
    summed = None
    for kernel_tap in range(5):
        tap_slice = lax.slice_in_dim(source, kernel_tap, kernel_tap + out_count, axis=conv_axis)
        tap_term = jnp.dot(
            tap_slice.reshape(-1, tap_slice.shape[-1]),
            weight[kernel_tap],
            preferred_element_type=jnp.float32,
        )
        summed = tap_term if summed is None else summed + tap_term
    out_shape = tuple(tap_slice.shape[:-1]) + (weight.shape[-1],)
    return summed.reshape(out_shape)


def pad_columns(source):
    return jnp.pad(source, ((0, 0), (2, 2), (0, 0)))


def rows_around(source, depth, mover):
    above = [
        mover(source, offset)
        for offset in list(range(depth, 0, -1)) + list(range(-1, -depth - 1, -1))
    ]
    return jnp.concatenate(above[:depth] + [source] + above[depth:], axis=0)


def row_pass(hidden, from_inputs, weight):
    width_h = hidden.shape[-1]
    hidden_half = lax.optimization_barrier(hidden.astype(jnp.bfloat16))
    gate_pair = jax.nn.sigmoid(
        conv_valid(pad_columns(hidden_half), weight[:, :width_h, : 2 * width_h], 1)
        + from_inputs[..., : 2 * width_h]
    )
    update_gate = gate_pair[..., :width_h]
    reset_gate = gate_pair[..., width_h:]
    gated = (reset_gate * hidden_half.astype(jnp.float32)).astype(jnp.bfloat16)
    candidate = jnp.tanh(
        conv_valid(pad_columns(gated), weight[:, :width_h, 2 * width_h :], 1)
        + from_inputs[..., 2 * width_h :]
    )
    return (1.0 - update_gate) * hidden + update_gate * candidate


def column_pass_each(hidden, from_inputs, weight):
    width_h = hidden.shape[-1]
    hidden_half = lax.optimization_barrier(hidden.astype(jnp.bfloat16))
    hidden_ext = rows_around(
        hidden_half, 2, lambda source, offset: passed_along(source, "band", offset)
    )
    gate_pair = jax.nn.sigmoid(
        conv_valid(hidden_ext, weight[:, :width_h, : 2 * width_h], 0)
        + from_inputs[..., : 2 * width_h]
    )
    update_gate = gate_pair[..., :width_h]
    reset_gate = gate_pair[..., width_h:]
    gated = (reset_gate * hidden_half.astype(jnp.float32)).astype(jnp.bfloat16)
    gated_ext = rows_around(gated, 2, lambda source, offset: passed_along(source, "band", offset))
    candidate = jnp.tanh(
        conv_valid(gated_ext, weight[:, :width_h, 2 * width_h :], 0)
        + from_inputs[..., 2 * width_h :]
    )
    return (1.0 - update_gate) * hidden + update_gate * candidate


def per_device_rows(frame1, frame2, context, hidden_init, offsets, w_motion, w_row, w_col):
    band_rows, image_width, channels = frame1.shape
    total_rows = band_rows * lax.axis_size("band")
    row_first = lax.axis_index("band") * band_rows
    strips = pool_strips(frame2)
    target_row, target_col, pixel_row, pixel_col = lookup_targets(
        offsets, row_first, total_rows, image_width
    )
    pixel_count = band_rows * image_width
    features = frame1.reshape(pixel_count, channels)
    rows_target = target_row.reshape(pixel_count)
    cols_target = target_col.reshape(pixel_count)
    zeros_state = jnp.zeros((pixel_count,), jnp.float32)
    initial = (
        jnp.full((pixel_count,), -jnp.inf, jnp.float32),
        zeros_state,
        zeros_state,
        zeros_state,
        zeros_state,
    )
    state = initial
    arriving = lax.all_gather(strips, "band", axis=0, tiled=True)
    arriving_rows = arriving.shape[0]
    step_rows = min(arriving_rows, 16)
    full_steps = arriving_rows // step_rows
    blocks = arriving.reshape((full_steps, step_rows) + arriving.shape[1:])
    starts = step_rows * jnp.arange(full_steps, dtype=jnp.int32)

    def advance(carry, pieces):
        return (
            strip_step(
                carry,
                features,
                pieces[0],
                pieces[1],
                total_rows,
                image_width,
                rows_target,
                cols_target,
            ),
            None,
        )

    state, unused = lax.scan(advance, state, (blocks, starts))
    running_max, denominator, acc_row, acc_col, lookup = state
    flow_row = (acc_row / denominator).reshape(band_rows, image_width) - pixel_row.astype(
        jnp.float32
    ) / total_rows
    flow_col = (acc_col / denominator).reshape(band_rows, image_width) - pixel_col.astype(
        jnp.float32
    ) / image_width
    lookup = lookup.reshape(band_rows, image_width)
    motion = jax.nn.relu(
        flow_row[..., None] * w_motion[0]
        + flow_col[..., None] * w_motion[1]
        + lookup[..., None] * w_motion[2]
    ).astype(jnp.bfloat16)
    inputs = jnp.concatenate([context, motion], axis=-1)
    width_h = hidden_init.shape[-1]
    from_row = conv_valid(pad_columns(inputs), w_row[:, width_h:, :], 1)
    hidden = hidden_init.astype(jnp.float32)
    inputs_ext = rows_around(inputs, 2, lambda source, offset: passed_along(source, "band", offset))
    from_col = conv_valid(inputs_ext, w_col[:, width_h:, :], 0)
    for iteration in range(ITERS):
        hidden = row_pass(hidden, from_row, w_row)
        hidden = column_pass_each(hidden, from_col, w_col)
    return (hidden, jnp.stack([flow_row, flow_col]))


BF = jnp.bfloat16
F32 = jnp.float32
MESH = pl.DeviceIdType.MESH
HALO = 4


def mm(a, b):
    return jnp.dot(a, b, preferred_element_type=F32)


def shifted_taps(padded, count):
    return jnp.concatenate(
        [padded[6 + k : 6 + k + count, :].astype(BF) for k in range(5)], axis=1
    )


def row_taps(value, step):
    zeros = jnp.zeros((2 * step, value.shape[1]), value.dtype)
    tall = jnp.concatenate([zeros, value, zeros], axis=0)
    count = value.shape[0]
    return jnp.concatenate([tall[k * step : k * step + count] for k in range(5)], axis=1)


def gate(x):
    return 0.5 * jnp.tanh(0.5 * x) + 0.5


def tap_weights(w_ref, first, low, high):
    return w_ref[:, first : first + 128, low:high].reshape(5 * 128, high - low)


def fused_kernel(
    bands,
    frame1_hbm,
    frame2_hbm,
    context_hbm,
    hidden_init_hbm,
    offsets_hbm,
    w_motion_hbm,
    w_row_hbm,
    w_col_hbm,
    hidden_out,
    flow_out,
    frame1,
    frame2,
    context,
    hidden_init,
    offsets,
    w_motion,
    w_row,
    w_col,
    strips,
    scores,
    ctx_stage,
    ctx_recv,
    flow_stage,
    flow_recv,
    hid_stage,
    hid_recv,
    out_stage,
    out_recv,
    pad_ctx,
    pad_hid,
    pad_mot,
    pad_gate,
    win_ctx,
    win_mot,
    win_hid,
    win_gate,
    acc_row,
    gate_row,
    acc_col,
    acc_row2,
    load_sem,
    strip_send,
    strip_recv,
    ctx_ssem,
    ctx_rsem,
    flow_ssem,
    flow_rsem,
    hid_ssem,
    hid_rsem,
    out_ssem,
    out_rsem,
):
    width = frame1.shape[0]
    own = width // bands
    win = own + 2 * HALO
    grid_cols = width // 8
    me = lax.axis_index("band")
    pair = lax.axis_index("pair")

    loads = [
        pltpu.make_async_copy(source, target, load_sem.at[i])
        for i, (source, target) in enumerate(
            (
                (frame2_hbm, frame2),
                (context_hbm, context),
                (hidden_init_hbm, hidden_init),
                (w_row_hbm, w_row),
                (frame1_hbm, frame1),
                (offsets_hbm, offsets),
                (w_motion_hbm, w_motion),
                (w_col_hbm, w_col),
            )
        )
    ]
    for load in loads:
        load.start()

    barrier = pltpu.get_barrier_semaphore()

    def greet(k, carry):
        pl.semaphore_signal(
            barrier, inc=1, device_id=(lax.rem(me + k, bands), pair), device_id_type=MESH
        )
        return carry

    lax.fori_loop(1, bands, greet, 0)

    loads[0].wait()
    blocks = frame2[...].astype(F32).reshape(grid_cols, 8, frame2.shape[1])
    strips[pl.ds(me, 1)] = (jnp.sum(blocks, axis=1) / 2.0).astype(BF)[None]

    def zero_ends(ref, count):
        ref[0:8, :] = jnp.zeros((8, 128), F32)
        ref[8 + count : 16 + count, :] = jnp.zeros((8, 128), F32)

    for ref in (pad_ctx, pad_hid, pad_mot, pad_gate):
        zero_ends(ref, width)
    for ref in (win_ctx, win_mot, win_hid, win_gate):
        zero_ends(ref, bands * win)

    loads[1].wait()
    loads[2].wait()
    pad_ctx[8 : 8 + width, :] = context[...].astype(F32)
    pad_hid[8 : 8 + width, :] = hidden_init[...].astype(F32)

    def stage_windows(stage, padded):
        for d in range(bands):
            first = 8 + own * d - HALO
            stage[d] = padded[first : first + win, :].astype(BF)

    stage_windows(ctx_stage, pad_ctx)

    order = sorted(range(1, bands), key=lambda k: abs(2 * k - bands))

    def scatter(stage, recv, ssem, rsem):
        for k in order:
            to = lax.rem(me + k, bands)
            pltpu.make_async_remote_copy(
                src_ref=stage.at[to],
                dst_ref=recv.at[me],
                send_sem=ssem,
                recv_sem=rsem,
                device_id=(to, pair),
                device_id_type=MESH,
            ).start()

    def wait_bytes(ref, sem):
        most = ref.at[pl.ds(0, bands - 1)]
        pltpu.make_async_copy(most, most, sem).wait()

    def collect(stage, recv, rsem):
        wait_bytes(recv, rsem)
        half = stage.shape[1] // 2 if stage.shape[1] == win else 0

        def keep(i, carry):
            recv[pl.ds(me, 1), pl.ds(i * half, half)] = stage[pl.ds(me, 1), pl.ds(i * half, half)]
            return carry

        if half:
            lax.fori_loop(0, 2, keep, 0)
        else:
            recv[pl.ds(me, 1)] = stage[pl.ds(me, 1)]

    def sent(stage, ssem):
        wait_bytes(stage, ssem)

    pl.semaphore_wait(barrier, bands - 1)

    level = me // 4
    place = lax.rem(me, 4)
    core = lax.rem(me, 2)
    sibling = me + 1 - 2 * core
    across = me + 2 - 4 * lax.rem(me // 2, 2)
    levels = (
        level,
        level + 1 - 2 * lax.rem(level, 2),
        2 - level // 2,
        3 - 3 * (level // 2),
    )
    line = [4 * other + place for other in levels]
    across_line = [4 * other + (across - 4 * level) for other in levels]
    started = []

    def pass_on(block, to, slot):
        copy = pltpu.make_async_remote_copy(
            src_ref=strips.at[block],
            dst_ref=strips.at[block],
            send_sem=strip_send.at[slot],
            recv_sem=strip_recv.at[block],
            device_id=(to, pair),
            device_id_type=MESH,
        )
        copy.start()
        started.append(copy)

    def arrived(block):
        pltpu.make_async_remote_copy(
            src_ref=strips.at[block],
            dst_ref=strips.at[block],
            send_sem=strip_send.at[0],
            recv_sem=strip_recv.at[block],
            device_id=(sibling, pair),
            device_id_type=MESH,
        ).wait_recv()

    pass_on(me, across, 1)
    pass_on(me, line[1], 0)
    pass_on(me, line[2], 2)
    pass_on(me, line[3], 3)
    pass_on(me, sibling, 4)

    loads[3].wait()
    gate_row[...] = mm(shifted_taps(pad_hid, width), tap_weights(w_row, 0, 0, 256))

    for i in (1, 2, 3):
        arrived(line[i])
        pass_on(line[i], across, 4 + i)
        pass_on(line[i], sibling, 7 + i)
    acc_row[...] = mm(shifted_taps(pad_ctx, width), tap_weights(w_row, 128, 0, 384))
    for i in (0, 1, 2, 3):
        arrived(across_line[i])
        pass_on(across_line[i], sibling, 11 + i)
    scatter(ctx_stage, ctx_recv, ctx_ssem, ctx_rsem)
    for load in loads[4:7]:
        load.wait()
    for i in (0, 1, 2, 3):
        arrived(line[i] + 1 - 2 * core)
    for i in (0, 1, 2, 3):
        arrived(across_line[i] + 1 - 2 * core)

    scores[...] = lax.dot_general(
        strips[...].reshape(bands * grid_cols, frame1.shape[1]),
        frame1[...],
        (((1,), (1,)), ((), ())),
        preferred_element_type=F32,
    ) * (1.0 / math.sqrt(frame1.shape[1]))

    row_f = me.astype(F32) / bands
    parts = []
    strip_ids = lax.broadcasted_iota(jnp.int32, (grid_cols, 128), 0)
    centres = ((8 * strip_ids).astype(F32) + 3.5) / width
    for lanes in range(0, width, 128):
        cut = slice(lanes, lanes + 128)
        column = lanes + lax.broadcasted_iota(jnp.int32, (1, 128), 1)
        target_row = me + offsets[0, :, cut]
        target_col = column // 8 + offsets[1, :, cut]
        inside = (
            (target_row >= 0)
            & (target_row < bands)
            & (target_col >= 0)
            & (target_col < grid_cols)
        )
        target = jnp.where(inside, target_row * grid_cols + target_col, -1)
        highest = scores[0:grid_cols, cut]
        for r in range(1, bands):
            highest = jnp.maximum(highest, scores[r * grid_cols : (r + 1) * grid_cols, cut])
        highest = jnp.max(highest, axis=0, keepdims=True)
        by_col = jnp.zeros((grid_cols, 128), F32)
        by_row = jnp.zeros((8, 128), F32)
        found = jnp.zeros((grid_cols, 128), F32)
        for r in range(bands):
            block = scores[r * grid_cols : (r + 1) * grid_cols, cut]
            raised = jnp.exp(block - highest)
            by_col = by_col + raised
            if r:
                folded = jnp.sum(raised.reshape(grid_cols // 8, 8, 128), axis=0)
                by_row = by_row + folded * (r / bands)
            found = found + jnp.where(strip_ids + r * grid_cols == target, block, 0.0)
        total = jnp.sum(by_col, axis=0, keepdims=True)
        moved_row = jnp.sum(by_row, axis=0, keepdims=True) / total
        moved_col = jnp.sum(by_col * centres, axis=0, keepdims=True) / total
        flow_row = moved_row - row_f
        flow_col = moved_col - column.astype(F32) / width
        flow_out[0, :, cut] = flow_row
        flow_out[1, :, cut] = flow_col
        parts.append(
            jnp.concatenate(
                [
                    flow_row,
                    flow_col,
                    jnp.sum(found, axis=0, keepdims=True),
                    jnp.zeros((5, 128), F32),
                ],
                axis=0,
            )
        )

    three = jnp.concatenate(parts + [jnp.zeros((8, 128), F32)], axis=1)
    span = width + 128
    line_id = lax.broadcasted_iota(jnp.int32, (8, span), 0)
    spread = jnp.where(line_id == 1, pltpu.roll(three, 32, 1), three)
    spread = jnp.where(line_id == 2, pltpu.roll(three, 64, 1), spread)
    lane_group = lax.broadcasted_iota(jnp.int32, (8, 128), 1) // 32
    wanted = lane_group == lax.broadcasted_iota(jnp.int32, (8, 128), 0)
    for d in range(bands):
        turned = pltpu.roll(spread, (span - (own * d - HALO)) % span, 1)[:, 0:128]
        flow_stage[d] = jnp.sum(jnp.where(wanted, turned, 0.0), axis=0, keepdims=True)
    scatter(flow_stage, flow_recv, flow_ssem, flow_rsem)

    def motion_of(first, second, third):
        return jnp.maximum(
            first * w_motion[0:1, :] + second * w_motion[1:2, :] + third * w_motion[2:3, :],
            0.0,
        )

    for i, part in enumerate(parts):
        upright = jnp.concatenate([part, jnp.zeros((120, 128), F32)], axis=0).T
        pad_mot[8 + 128 * i : 136 + 128 * i, :] = motion_of(
            upright[:, 0:1], upright[:, 1:2], upright[:, 2:3]
        )
    acc = mm(shifted_taps(pad_mot, width), tap_weights(w_row, 256, 0, 384)) + acc_row[...]
    start = pad_hid[8 : 8 + width, :]
    update = gate(gate_row[:, 0:128] + acc[:, 0:128])
    reset = gate(gate_row[:, 128:256] + acc[:, 128:256])
    pad_gate[8 : 8 + width, :] = reset * start
    candidate = jnp.tanh(
        mm(shifted_taps(pad_gate, width), tap_weights(w_row, 0, 256, 384)) + acc[:, 256:384]
    )
    pad_hid[8 : 8 + width, :] = (1.0 - update) * start + update * candidate
    stage_windows(hid_stage, pad_hid)
    scatter(hid_stage, hid_recv, hid_ssem, hid_rsem)

    pixels = bands * win
    collect(ctx_stage, ctx_recv, ctx_rsem)
    loads[7].wait()
    ctx = ctx_recv[...].reshape(pixels, 128)
    win_ctx[8 : 8 + pixels, :] = ctx.astype(F32)
    ctx_down = row_taps(ctx, win)
    ctx_along = shifted_taps(win_ctx, pixels)
    collect(flow_stage, flow_recv, flow_rsem)
    upright = jnp.concatenate(
        [flow_recv[r] for r in range(bands)] + [jnp.zeros((128 - bands, 128), F32)], axis=0
    ).T
    for r in range(bands):
        win_mot[8 + win * r : 8 + win * (r + 1), :] = motion_of(
            upright[0:win, r : r + 1],
            upright[win : 2 * win, r : r + 1],
            upright[2 * win : 3 * win, r : r + 1],
        )
    motion = win_mot[8 : 8 + pixels, :].astype(BF)
    for acc_ref, weight, both in (
        (acc_col, w_col, (ctx_down, row_taps(motion, win))),
        (acc_row2, w_row, (ctx_along, shifted_taps(win_mot, pixels))),
    ):
        acc_ref[...] = mm(
            jnp.concatenate(both, axis=1),
            jnp.concatenate(
                [tap_weights(weight, 128, 0, 384), tap_weights(weight, 256, 0, 384)], axis=0
            ),
        )

    collect(hid_stage, hid_recv, hid_rsem)
    state_half = hid_recv[...].reshape(pixels, 128)
    state = state_half.astype(F32)

    def gru(state, half, acc, weight, taps_of):
        pre = mm(taps_of(half, win_hid), tap_weights(weight, 0, 0, 256)) + acc[:, 0:256]
        update = gate(pre[:, 0:128])
        reset = gate(pre[:, 128:256])
        gated = (reset * half.astype(F32)).astype(BF)
        candidate = jnp.tanh(
            mm(taps_of(gated, win_gate), tap_weights(weight, 0, 256, 384)) + acc[:, 256:384]
        )
        return (1.0 - update) * state + update * candidate

    def taps_down(value, unused):
        return row_taps(value, win)

    def taps_along(value, padded):
        padded[8 : 8 + pixels, :] = value.astype(F32)
        return shifted_taps(padded, pixels)

    state = gru(state, state_half, acc_col, w_col, taps_down)
    state = gru(state, state.astype(BF), acc_row2, w_row, taps_along)
    state = gru(state, state.astype(BF), acc_col, w_col, taps_down)
    win_hid[8 : 8 + pixels, :] = state
    for r in range(bands):
        first = 8 + win * r + HALO
        out_stage[r] = win_hid[first : first + own, :].astype(BF)
    scatter(out_stage, out_recv, out_ssem, out_rsem)
    for copy in started:
        copy.wait_send()
    sent(ctx_stage, ctx_ssem)
    sent(flow_stage, flow_ssem)
    sent(hid_stage, hid_ssem)
    collect(out_stage, out_recv, out_rsem)
    hidden_out[...] = out_recv[...]
    sent(out_stage, out_ssem)


def per_device_columns(
    bands, frame1, frame2, context, hidden_init, offsets, w_motion, w_row, w_col
):
    unused, width, channels = frame1.shape
    own = width // bands
    win = own + 2 * HALO
    pixels = bands * win
    vmem = pl.BlockSpec(memory_space=pltpu.VMEM)
    hbm = pl.BlockSpec(memory_space=pltpu.HBM)
    dma = pltpu.SemaphoreType.DMA
    tall = pltpu.VMEM((width + 16, 128), F32)
    wide = pltpu.VMEM((pixels + 16, 128), F32)
    hidden, flow = pl.pallas_call(
        functools.partial(fused_kernel, bands),
        out_shape=(
            jax.ShapeDtypeStruct((bands, own, 128), BF),
            jax.ShapeDtypeStruct((2, 1, width), F32),
        ),
        in_specs=[hbm] * 8,
        out_specs=(vmem, vmem),
        scratch_shapes=[
            pltpu.VMEM((width, channels), BF),
            pltpu.VMEM((width, channels), BF),
            pltpu.VMEM((width, 128), BF),
            pltpu.VMEM((width, 128), BF),
            pltpu.VMEM(offsets.shape, jnp.int32),
            pltpu.VMEM(w_motion.shape, F32),
            pltpu.VMEM(w_row.shape, BF),
            pltpu.VMEM(w_col.shape, BF),
            pltpu.VMEM((bands, width // 8, channels), BF),
            pltpu.VMEM((bands * width // 8, width), F32),
            pltpu.VMEM((bands, win, 128), BF),
            pltpu.VMEM((bands, win, 128), BF),
            pltpu.VMEM((bands, 1, 128), F32),
            pltpu.VMEM((bands, 1, 128), F32),
            pltpu.VMEM((bands, win, 128), BF),
            pltpu.VMEM((bands, win, 128), BF),
            pltpu.VMEM((bands, own, 128), BF),
            pltpu.VMEM((bands, own, 128), BF),
            tall,
            tall,
            tall,
            tall,
            wide,
            wide,
            wide,
            wide,
            pltpu.VMEM((width, 384), F32),
            pltpu.VMEM((width, 256), F32),
            pltpu.VMEM((pixels, 384), F32),
            pltpu.VMEM((pixels, 384), F32),
            dma((8,)),
            dma((15,)),
            dma((bands,)),
        ]
        + [dma] * 8,
        compiler_params=pltpu.CompilerParams(
            collective_id=0, has_side_effects=True, vmem_limit_bytes=63 * 1024 * 1024
        ),
        cost_estimate=pl.CostEstimate(
            flops=2_400_000_000, bytes_accessed=4_500_000, transcendentals=700_000
        ),
    )(
        frame1.reshape(width, channels),
        frame2.reshape(width, channels),
        context.reshape(width, 128),
        hidden_init.reshape(width, 128),
        offsets,
        w_motion,
        w_row,
        w_col,
    )
    return (hidden.astype(F32).reshape(1, width, 128), flow)


def solution(mesh):
    bands = mesh.shape["band"]

    def per_device(frame1, frame2, *rest):
        own = frame1.shape[1] // bands
        if bands == 16 and frame1.shape[0] == 1 and own + 2 * HALO == 32:
            return per_device_columns(bands, frame1, frame2, *rest)
        return per_device_rows(frame1, frame2, *rest)

    return jax.shard_map(
        per_device,
        mesh=mesh,
        in_specs=(
            P("band", "pair", None),
            P("band", "pair", None),
            P("band", "pair", None),
            P("band", "pair", None),
            P(None, "band", "pair"),
            P(),
            P(),
            P(),
        ),
        out_specs=(P("band", "pair", None), P(None, "band", "pair")),
        check_vma=False,
    )
```
